32 devices in a mesh: groups: 2 (over y), sector: 8 (over z, x), term: 2 (over core).
Axes of the slice: x: 2, y: 2, z: 4, core: 2. Of those that a mesh axis runs over, the one named last changes fastest.
Arguments:
- psi_tiles: bfloat16 [16, 16, 256, 128], P(('groups', 'sector')), parts along dimension 0, may hold values from -6 to 6
- env_left: bfloat16 [16, 34, 256, 256], P(('groups', 'sector'), 'term'), parts along dimension 0, may hold values from -0.375 to 0.375
- env_right: bfloat16 [16, 34, 128, 128], P(('groups', 'sector'), 'term'), parts along dimension 0, may hold values from -0.5 to 0.5
- mpo_local: bfloat16 [68, 16, 16], P(('groups', 'term')), parts along dimension 0, may hold values from -0.25 to 0.25
- term_class: int32 [68], P(('groups', 'term')), parts along dimension 0, may hold values from 0 to 4
Outputs:
- h_psi: bfloat16 [16, 16, 256, 128], P(('groups', 'sector'), 'term'), parts along dimension 0
The draws below stay inside these ranges and needn't reach their ends.
There are 2 independent parts, one for each index of `groups`. The reference program is written for one: setup_inputs(seed, part) draws one part's arguments, and reference() takes and returns one part's arrays. A program takes and returns all parts, laid end to end along the dimension named above; each array names one. Nothing has to cross between parts.
All inputs are finite; a program needn't handle non-finite values.
Results may differ from the reference program's by a relative error of at most 0.0057.
Values may be sent and summed in bfloat16 or wider, within the bound.
A program may use at most 64 MiB of HBM per device.

```python
import jax
import jax.numpy as jnp
from jax import lax

PH = 16
TERMS = 34
DR = 128
DL = 256
GRID = 4
SECTORS = 8


def place_ends(result, key, smallest, top_value):
    spot = [jax.random.randint(jax.random.fold_in(key, axis), (), 0, length) for axis, length in enumerate(result.shape)]
    main_axis = result.shape.index(max(result.shape))
    next_to = spot[:main_axis] + [(spot[main_axis] + 1) % result.shape[main_axis]] + spot[main_axis + 1:]
    return result.at[tuple(spot)].set(smallest).at[tuple(next_to)].set(top_value)


def levels(stream_key, shape, split, smallest, largest):
    level, own = 1.0, jax.random.fold_in(stream_key, 6)
    for axis_at, blocks in split:
        draws = jnp.exp(jax.random.uniform(jax.random.fold_in(own, axis_at), (blocks,), jnp.float32, smallest / len(split), largest / len(split)))
        level = level * jnp.repeat(draws, shape[axis_at] // blocks).reshape([-1 if axis == axis_at else 1 for axis in range(len(shape))])
    return level


def centred(rng, extent, spread, limit, split=(), held_as=jnp.bfloat16):
    entries = spread * jax.random.normal(rng, extent, jnp.float32)
    if split:
        entries = entries * levels(rng, extent, split, -0.22, 0.18)
    return jnp.clip(entries, -limit, limit).astype(held_as)


def setup_inputs(seed: int = 0, part: int = 0) -> dict:
    streams_of = jax.random.split(jax.random.key(seed), 6)
    own_keys = jax.random.split(jax.random.fold_in(streams_of[5], part), 6)
    psi_tiles = centred(own_keys[0], (SECTORS, PH, DL, DR), 1.0, 6.0, ((0, 8),))
    env_left = centred(own_keys[1], (SECTORS, TERMS, DL, DL), DL ** -0.5, 0.375, ((0, 8), (1, 2)))
    env_right = centred(own_keys[2], (SECTORS, TERMS, DR, DR), DR ** -0.5, 0.5, ((0, 8), (1, 2)))
    mpo_local = centred(own_keys[3], (TERMS, PH, PH), (PH * TERMS) ** -0.5, 0.25, ((0, 2),))
    term_class = place_ends(jax.random.randint(own_keys[4], (TERMS,), 0, 5), jax.random.fold_in(own_keys[4], 1), 0, 4).astype(jnp.int32)
    return {"psi_tiles": psi_tiles, "env_left": env_left, "env_right": env_right, "mpo_local": mpo_local, "term_class": term_class}


def neighbours(psi_tiles):
    zero_one = jnp.zeros_like(psi_tiles[:1])
    zero_row = jnp.zeros_like(psi_tiles[:GRID])
    column = (jnp.arange(SECTORS) + 1) % GRID
    before = jnp.concatenate([zero_one, psi_tiles[:-1]], 0)
    after = jnp.concatenate([psi_tiles[1:], zero_one], 0)
    before = jnp.where((column > 0)[:, None, None, None], before, jnp.zeros_like(before))
    after = jnp.where((column < GRID - 1)[:, None, None, None], after, jnp.zeros_like(after))
    lower = jnp.concatenate([zero_row, psi_tiles[:-GRID]], 0)
    upper = jnp.concatenate([psi_tiles[GRID:], zero_row], 0)
    return jnp.stack([psi_tiles, before, after, lower, upper], 1)


def one_sector(inputs, mpo_local, term_class):
    candidates, lefts, rights = inputs

    def add_term(total, index):
        source = lax.dynamic_index_in_dim(candidates, term_class[index], 0, keepdims=False)
        right_part = jnp.dot(source.reshape(PH * DL, DR), rights[index], preferred_element_type=jnp.float32)
        right_part = right_part.astype(jnp.bfloat16).reshape(PH, DL * DR)
        mixed = jnp.dot(mpo_local[index], right_part, preferred_element_type=jnp.float32)
        mixed = mixed.astype(jnp.bfloat16).reshape(PH, DL, DR)
        term_part = jnp.einsum("ij,pjk->pik", lefts[index].astype(jnp.float32), mixed.astype(jnp.float32))
        return total + term_part, None

    start = jnp.zeros((PH, DL, DR), jnp.float32)
    total, unused = lax.scan(add_term, start, jnp.arange(TERMS, dtype=jnp.int32))
    return total.astype(jnp.bfloat16)


def reference(psi_tiles, env_left, env_right, mpo_local, term_class):
    candidates = neighbours(psi_tiles)
    return lax.map(lambda inputs: one_sector(inputs, mpo_local, term_class), (candidates, env_left, env_right))
```

```python
import functools

import jax
import jax.numpy as jnp
from jax import lax
from jax.experimental import pallas as pl
from jax.experimental.pallas import tpu as pltpu
from jax.sharding import PartitionSpec as P

GRID = 4
MESH = pl.DeviceIdType.MESH
STEPS = (-1, 1, -GRID, GRID)
VMEM_LIMIT = 56 * 1024 * 1024


def has_source(sector, sectors, step):
    column = lax.rem(sector + 1, GRID)
    if step == -1:
        return (sector >= 1) & (column > 0)
    if step == 1:
        return (sector + 1 < sectors) & (column < GRID - 1)
    if step < 0:
        return sector + step >= 0
    return sector + step < sectors


def exchange_kernel(sectors, psi_ref, out_ref, send_sem, recv_sem, pass_sem, got_sem):
    group, sector, core = (lax.axis_index(name) for name in ("groups", "sector", "term"))
    half = psi_ref.shape[0] // 2
    mine = pl.ds(core * half, half)
    barrier = pltpu.get_barrier_semaphore()
    sibling = (group, sector, 1 - core)
    count = jnp.int32(1)
    pl.semaphore_signal(barrier, inc=1, device_id=sibling, device_id_type=MESH)
    for step in STEPS:
        there = has_source(sector, sectors, step)
        count = count + there.astype(jnp.int32)

        @pl.when(there)
        def _():
            pl.semaphore_signal(barrier, inc=1, device_id=(group, sector + step, core), device_id_type=MESH)

    pl.semaphore_wait(barrier, count)

    def outgoing(slot):
        step = STEPS[slot]
        return pltpu.make_async_remote_copy(
            src_ref=psi_ref.at[mine],
            dst_ref=out_ref.at[slot, mine],
            send_sem=send_sem.at[slot],
            recv_sem=recv_sem.at[slot],
            device_id=(group, sector - step, core),
            device_id_type=MESH,
        )

    def passing(slot):
        return pltpu.make_async_remote_copy(
            src_ref=out_ref.at[slot, mine],
            dst_ref=out_ref.at[slot, mine],
            send_sem=pass_sem.at[slot],
            recv_sem=got_sem.at[slot],
            device_id=sibling,
            device_id_type=MESH,
        )

    there = [has_source(sector, sectors, step) for step in STEPS]
    wanted = [has_source(sector, sectors, -step) for step in STEPS]
    for slot in range(len(STEPS)):
        pl.when(wanted[slot])(lambda slot=slot: outgoing(slot).start())
    for slot in range(len(STEPS)):

        @pl.when(there[slot])
        def _():
            outgoing(slot).wait_recv()
            passing(slot).start()

    for slot in range(len(STEPS)):

        @pl.when(there[slot])
        def _():
            passing(slot).wait()

        pl.when(wanted[slot])(lambda slot=slot: outgoing(slot).wait_send())


def exchange(psi, sectors):
    slots = len(STEPS)
    return pl.pallas_call(
        functools.partial(exchange_kernel, sectors),
        out_shape=jax.ShapeDtypeStruct((slots, *psi.shape), psi.dtype),
        in_specs=[pl.BlockSpec(memory_space=pl.ANY)],
        out_specs=pl.BlockSpec(memory_space=pl.ANY),
        scratch_shapes=[pltpu.SemaphoreType.DMA((slots,))] * 4,
        compiler_params=pltpu.CompilerParams(collective_id=0, has_side_effects=True, vmem_limit_bytes=VMEM_LIMIT),
        name="exchange",
    )(psi)


def add_pair(xs, rights, mpos, lefts, scales, held, mixed, acc, first):
    states, rows, width = acc.shape
    step = 16
    wide = states * step
    index = lambda axis: lax.broadcasted_iota(jnp.int32, (wide, wide), axis)
    same = lax.rem(index(0), step) == lax.rem(index(1), step)
    spread = (lax.broadcasted_iota(jnp.int32, (wide, states), 0) // step
              == lax.broadcasted_iota(jnp.int32, (wide, states), 1)).astype(jnp.bfloat16)
    spread_t = (lax.broadcasted_iota(jnp.int32, (states, wide), 1) // step
                == lax.broadcasted_iota(jnp.int32, (states, wide), 0)).astype(jnp.bfloat16)

    def dot(a, b):
        return jnp.dot(a, b, preferred_element_type=jnp.float32)

    krons = []
    for mpo, scale in zip(mpos, scales):
        tall = dot(spread, mpo).astype(jnp.bfloat16)
        krons.append(jnp.where(same, dot(tall, spread_t) * scale, 0.0).astype(jnp.bfloat16))
    zero = jnp.zeros((width, width), jnp.bfloat16)
    right = jnp.concatenate(
        [jnp.concatenate([rights[0], zero], 1), jnp.concatenate([zero, rights[1]], 1)], 0
    )
    for s in range(0, states, 2):
        x = jnp.concatenate([x(s).reshape(2 * rows, width) for x in xs], 1)
        held[pl.ds(s, 2)] = dot(x, right).astype(jnp.bfloat16).reshape(2, rows, 2 * width)
    for t in range(2):
        for r in range(0, rows, 2 * step):
            part = [
                held[:, pl.ds(r + o, step), pl.ds(t * width, width)].reshape(wide, width) for o in (0, step)
            ]
            out = dot(krons[t], jnp.concatenate(part, 1)).astype(jnp.bfloat16)
            for n, o in enumerate((0, step)):
                mixed[t, :, pl.ds(r + o, step), :] = out[:, n * width:(n + 1) * width].reshape(states, step, width)
    left = jnp.concatenate(lefts, 1)
    for s in range(0, states, 2):
        part = [jnp.concatenate([mixed[t, s], mixed[t, s + 1]], 1) for t in range(2)]
        out = dot(left, jnp.concatenate(part, 0))
        for n in range(2):
            acc[s + n] += out[:, n * width:(n + 1) * width]


def terms_kernel(plan_ref, scale_ref, psi_ref, got_ref, left_ref, right_ref, mpo_ref, out_ref,
                 tiles, lefts, acc, held, mixed, sems):
    terms = left_ref.shape[0]
    copies = [
        pltpu.make_async_copy(psi_ref, tiles.at[0], sems.at[0]),
        pltpu.make_async_copy(got_ref, tiles.at[pl.ds(1, got_ref.shape[0])], sems.at[1]),
        pltpu.make_async_copy(left_ref, lefts, sems.at[2]),
    ]
    for copy in copies:
        copy.start()
    acc[...] = jnp.zeros_like(acc)
    for copy in copies:
        copy.wait()
    pairs = plan_ref[2, 0]

    @pl.loop(0, pairs)
    def _(pair):
        term = [plan_ref[0, 2 * pair + t] for t in range(2)]
        kind = [plan_ref[1, 2 * pair + t] for t in range(2)]
        add_pair(
            [lambda s, k=k: tiles[k, pl.ds(s, 2)] for k in kind],
            [right_ref[i] for i in term],
            [mpo_ref[i] for i in term],
            [lefts[i] for i in term],
            [scale_ref[2 * pair + t] for t in range(2)],
            held, mixed, acc, None,
        )

    out_ref[...] = acc[...]


def all_terms(plan, scale, psi, got, left, right, mpo):
    states, rows, width = psi.shape
    slots = got.shape[0]
    any_spec = pl.BlockSpec(memory_space=pl.ANY)
    smem = pl.BlockSpec(memory_space=pltpu.SMEM)
    vmem = pl.BlockSpec(memory_space=pltpu.VMEM)
    return pl.pallas_call(
        terms_kernel,
        out_shape=jax.ShapeDtypeStruct(psi.shape, jnp.float32),
        in_specs=[smem, smem, any_spec, any_spec, any_spec, vmem, vmem],
        out_specs=vmem,
        scratch_shapes=[
            pltpu.VMEM((slots + 1, states, rows, width), jnp.bfloat16),
            pltpu.VMEM(left.shape, jnp.bfloat16),
            pltpu.VMEM((states, rows, width), jnp.float32),
            pltpu.VMEM((states, rows, 2 * width), jnp.bfloat16),
            pltpu.VMEM((2, states, rows, width), jnp.bfloat16),
            pltpu.SemaphoreType.DMA((3,)),
        ],
        compiler_params=pltpu.CompilerParams(vmem_limit_bytes=VMEM_LIMIT),
        name="terms",
    )(plan, scale, psi, got, left, right, mpo)


def join_kernel(total_ref, out_ref, inbox, sems):
    group, sector, core = (lax.axis_index(name) for name in ("groups", "sector", "term"))
    half = out_ref.shape[0]
    sibling = (group, sector, 1 - core)
    barrier = pltpu.get_barrier_semaphore()
    pl.semaphore_signal(barrier, inc=1, device_id=sibling, device_id_type=MESH)
    pl.semaphore_wait(barrier, 1)
    copy = pltpu.make_async_remote_copy(
        src_ref=total_ref.at[pl.ds((1 - core) * half, half)],
        dst_ref=inbox,
        send_sem=sems.at[0],
        recv_sem=sems.at[1],
        device_id=sibling,
        device_id_type=MESH,
    )
    copy.start()
    copy.wait()
    out_ref[...] = (total_ref[pl.ds(core * half, half)] + inbox[...]).astype(out_ref.dtype)


def joined(total):
    states, rows, width = total.shape
    return pl.pallas_call(
        join_kernel,
        out_shape=jax.ShapeDtypeStruct((states // 2, rows, width), jnp.bfloat16),
        in_specs=[pl.BlockSpec(memory_space=pltpu.VMEM)],
        out_specs=pl.BlockSpec(memory_space=pltpu.VMEM),
        scratch_shapes=[
            pltpu.VMEM((states // 2, rows, width), jnp.float32),
            pltpu.SemaphoreType.DMA((2,)),
        ],
        compiler_params=pltpu.CompilerParams(collective_id=1, has_side_effects=True, vmem_limit_bytes=VMEM_LIMIT),
        name="join",
    )(total)


def planned(term_class, sectors):
    sector = lax.axis_index("sector")
    there = jnp.stack([jnp.bool_(True)] + [has_source(sector, sectors, step) for step in STEPS])
    kinds = jnp.arange(len(STEPS) + 1)
    exists = jnp.any((term_class[:, None] == kinds) & there, 1)
    count = term_class.shape[0]
    number = jnp.arange(count)
    key = jnp.where(exists, term_class, len(STEPS) + 1) * count + number
    rank = jnp.sum(key[None, :] < key[:, None], 1)
    valid = jnp.sum(exists.astype(jnp.int32))
    place = jnp.arange(count + 1)
    at = (rank[None, :] == place[:, None]) & exists
    term = jnp.sum(jnp.where(at, number, 0), 1)
    kind = jnp.sum(jnp.where(at, term_class, 0), 1)
    pairs = jnp.broadcast_to((valid + 1) // 2, place.shape)
    plan = jnp.stack([term, kind, pairs]).astype(jnp.int32)
    return plan, (place < valid).astype(jnp.float32)


def shards(psi_tiles, env_left, env_right, mpo_local, term_class):
    sectors = lax.axis_size("sector")
    plan, scale = planned(term_class, sectors)
    got = exchange(psi_tiles[0], sectors)
    total = all_terms(plan, scale, psi_tiles[0], got, env_left[0], env_right[0], mpo_local)
    return joined(total)[None]


def solution(mesh):
    placed = (
        P(("groups", "sector"), None, None, None),
        P(("groups", "sector"), "term", None, None),
        P(("groups", "sector"), "term", None, None),
        P(("groups", "term"), None, None),
        P(("groups", "term")),
    )
    return jax.shard_map(
        shards,
        mesh=mesh,
        in_specs=placed,
        out_specs=P(("groups", "sector"), "term", None, None),
        check_vma=False,
    )
```

```python
import functools

import jax
import jax.numpy as jnp
from jax import lax
from jax.experimental import pallas as pl
from jax.experimental.pallas import tpu as pltpu
from jax.sharding import PartitionSpec as P

GRID = 4
MESH = pl.DeviceIdType.MESH
STEPS = (-1, 1, -GRID, GRID)
FRONT_KINDS, FRONT_SLOTS = 3, 6
VMEM_LIMIT = 56 * 1024 * 1024


def has_source(sector, sectors, step):
    column = lax.rem(sector + 1, GRID)
    if step == -1:
        return (sector >= 1) & (column > 0)
    if step == 1:
        return (sector + 1 < sectors) & (column < GRID - 1)
    if step < 0:
        return sector + step >= 0
    return sector + step < sectors


def add_pair(xs, rights, mpos, lefts, scales, held, mixed, acc):
    states, rows, width = acc.shape
    step = 16
    wide = states * step
    index = lambda axis: lax.broadcasted_iota(jnp.int32, (wide, wide), axis)
    same = lax.rem(index(0), step) == lax.rem(index(1), step)
    spread = (lax.broadcasted_iota(jnp.int32, (wide, states), 0) // step
              == lax.broadcasted_iota(jnp.int32, (wide, states), 1)).astype(jnp.bfloat16)
    spread_t = (lax.broadcasted_iota(jnp.int32, (states, wide), 1) // step
                == lax.broadcasted_iota(jnp.int32, (states, wide), 0)).astype(jnp.bfloat16)

    def dot(a, b):
        return jnp.dot(a, b, preferred_element_type=jnp.float32)

    krons = []
    for mpo, scale in zip(mpos, scales):
        tall = dot(spread, mpo).astype(jnp.bfloat16)
        krons.append(jnp.where(same, dot(tall, spread_t) * scale, 0.0).astype(jnp.bfloat16))
    zero = jnp.zeros((width, width), jnp.bfloat16)
    right = jnp.concatenate(
        [jnp.concatenate([rights[0], zero], 1), jnp.concatenate([zero, rights[1]], 1)], 0
    )
    for s in range(0, states, 2):
        x = jnp.concatenate([x(s).reshape(2 * rows, width) for x in xs], 1)
        held[pl.ds(s, 2)] = dot(x, right).astype(jnp.bfloat16).reshape(2, rows, 2 * width)
    for t in range(2):
        for r in range(0, rows, 2 * step):
            part = [
                held[:, pl.ds(r + o, step), pl.ds(t * width, width)].reshape(wide, width) for o in (0, step)
            ]
            out = dot(krons[t], jnp.concatenate(part, 1)).astype(jnp.bfloat16)
            for n, o in enumerate((0, step)):
                mixed[t, :, pl.ds(r + o, step), :] = out[:, n * width:(n + 1) * width].reshape(states, step, width)
    left = jnp.concatenate(lefts, 1)
    for s in range(0, states, 2):
        part = [jnp.concatenate([mixed[t, s], mixed[t, s + 1]], 1) for t in range(2)]
        out = dot(left, jnp.concatenate(part, 0))
        for n in range(2):
            acc[s + n] += out[:, n * width:(n + 1) * width]


def front_kernel(sectors, class_ref, psi_ref, left_ref, right_ref, mpo_ref, got_ref, acc,
                 tiles, lefts, rights, held, mixed, plan, send_sem, recv_sem, pass_sem, got_sem, local_sem):
    group, sector, core = (lax.axis_index(name) for name in ("groups", "sector", "term"))
    half = psi_ref.shape[0] // 2
    terms = left_ref.shape[0]
    mine = pl.ds(core * half, half)
    barrier = pltpu.get_barrier_semaphore()
    sibling = (group, sector, 1 - core)
    there = [has_source(sector, sectors, step) for step in STEPS]
    wanted = [has_source(sector, sectors, -step) for step in STEPS]
    count = jnp.int32(1)
    pl.semaphore_signal(barrier, inc=1, device_id=sibling, device_id_type=MESH)
    for slot, step in enumerate(STEPS):
        count = count + there[slot].astype(jnp.int32)

        @pl.when(there[slot])
        def _():
            pl.semaphore_signal(barrier, inc=1, device_id=(group, sector + step, core), device_id_type=MESH)

    pl.semaphore_wait(barrier, count)

    def outgoing(slot):
        return pltpu.make_async_remote_copy(
            src_ref=psi_ref.at[mine],
            dst_ref=got_ref.at[slot, mine],
            send_sem=send_sem.at[slot],
            recv_sem=recv_sem.at[slot],
            device_id=(group, sector - STEPS[slot], core),
            device_id_type=MESH,
        )

    def passing(slot):
        return pltpu.make_async_remote_copy(
            src_ref=got_ref.at[slot, mine],
            dst_ref=got_ref.at[slot, mine],
            send_sem=pass_sem.at[slot],
            recv_sem=got_sem.at[slot],
            device_id=sibling,
            device_id_type=MESH,
        )

    def arrive(slot):
        @pl.when(there[slot])
        def _():
            outgoing(slot).wait_recv()
            passing(slot).start()

    def load(slot):
        @pl.when(there[slot])
        def _():
            passing(slot).wait()
            copy = pltpu.make_async_copy(got_ref.at[slot], tiles.at[slot + 1], local_sem.at[3])
            copy.start()
            copy.wait()

    for slot in range(len(STEPS)):
        pl.when(wanted[slot])(lambda slot=slot: outgoing(slot).start())
    copies = [
        pltpu.make_async_copy(psi_ref, tiles.at[0], local_sem.at[0]),
        pltpu.make_async_copy(left_ref, lefts, local_sem.at[1]),
        pltpu.make_async_copy(right_ref, rights, local_sem.at[2]),
    ]
    for copy in copies:
        copy.start()

    def note(index, state):
        fresh = []
        for kind, (found, slots) in enumerate(state):
            match = class_ref[index] == kind
            slots = tuple(jnp.where(match & (found == n), index, slot) for n, slot in enumerate(slots))
            fresh.append((found + match.astype(jnp.int32), slots))
        return tuple(fresh)

    zero = jnp.int32(0)
    state = lax.fori_loop(0, terms, note, tuple((zero, (zero,) * FRONT_SLOTS) for _ in range(FRONT_KINDS)))
    for kind, (found, slots) in enumerate(state):
        for n, slot in enumerate(slots):
            plan[0, kind * FRONT_SLOTS + n] = slot
            plan[1, kind * FRONT_SLOTS + n] = (n < found).astype(jnp.int32)
    acc[...] = jnp.zeros_like(acc)
    for copy in copies:
        copy.wait()

    @pl.loop(0, FRONT_KINDS)
    def _(phase):
        @pl.when(phase == 1)
        def _():
            arrive(0)
            arrive(1)
            load(0)

        @pl.when(phase == 2)
        def _():
            load(1)

        live = (phase == 0) | ((phase == 1) & there[0]) | ((phase == 2) & there[1])

        @pl.when(live)
        def _():
            @pl.loop(0, FRONT_SLOTS // 2)
            def _(pair):
                spot = [phase * FRONT_SLOTS + 2 * pair + t for t in range(2)]
                term = [plan[0, n] for n in spot]
                add_pair(
                    [lambda s: tiles[phase, pl.ds(s, 2)]] * 2,
                    [rights[i] for i in term],
                    [mpo_ref[i] for i in term],
                    [lefts[i] for i in term],
                    [plan[1, n].astype(jnp.float32) for n in spot],
                    held, mixed, acc,
                )

    for slot in (2, 3):
        arrive(slot)
    for slot in range(len(STEPS)):
        if slot >= 2:
            pl.when(there[slot])(lambda slot=slot: passing(slot).wait())
        pl.when(wanted[slot])(lambda slot=slot: outgoing(slot).wait_send())


SMEM_SPEC = pl.BlockSpec(memory_space=pltpu.SMEM)
VMEM_SPEC = pl.BlockSpec(memory_space=pltpu.VMEM)
ANY_SPEC = pl.BlockSpec(memory_space=pl.ANY)


def front(term_class, psi, left, right, mpo, sectors):
    states, rows, width = psi.shape
    slots = len(STEPS)
    return pl.pallas_call(
        functools.partial(front_kernel, sectors),
        out_shape=(
            jax.ShapeDtypeStruct((slots, *psi.shape), psi.dtype),
            jax.ShapeDtypeStruct(psi.shape, jnp.float32),
        ),
        in_specs=[SMEM_SPEC, ANY_SPEC, ANY_SPEC, ANY_SPEC, VMEM_SPEC],
        out_specs=(ANY_SPEC, VMEM_SPEC),
        scratch_shapes=[
            pltpu.VMEM((FRONT_KINDS, states, rows, width), jnp.bfloat16),
            pltpu.VMEM(left.shape, jnp.bfloat16),
            pltpu.VMEM(right.shape, jnp.bfloat16),
            pltpu.VMEM((states, rows, 2 * width), jnp.bfloat16),
            pltpu.VMEM((2, states, rows, width), jnp.bfloat16),
            pltpu.SMEM((2, FRONT_KINDS * FRONT_SLOTS), jnp.int32),
        ] + [pltpu.SemaphoreType.DMA((slots,))] * 5,
        compiler_params=pltpu.CompilerParams(collective_id=0, has_side_effects=True, vmem_limit_bytes=VMEM_LIMIT),
        name="front",
    )(term_class, psi, left, right, mpo)


def rest_kernel(sectors, class_ref, psi_ref, got_ref, left_ref, right_ref, mpo_ref, total_ref, own_ref, sent_ref,
                tiles, lefts, rights, acc, held, mixed, plan, tile_sem, left_sem, right_sem, acc_sem):
    sector, core = lax.axis_index("sector"), lax.axis_index("term")
    terms = left_ref.shape[0]
    states = acc.shape[0]
    start = pltpu.make_async_copy(total_ref, acc, acc_sem)
    start.start()
    used = jnp.int32(0)
    need = []
    for kind in range(len(STEPS) + 1):
        there = jnp.bool_(True) if kind == 0 else has_source(sector, sectors, STEPS[kind - 1])
        skip = FRONT_SLOTS if kind < FRONT_KINDS else 0
        before = used

        def note(index, state, kind=kind, there=there, skip=skip):
            used, found = state
            match = (class_ref[index] == kind) & there
            plan[0, used] = index
            plan[1, used] = kind
            take = match & (found >= skip)
            return used + take.astype(jnp.int32), found + match.astype(jnp.int32)

        used, found = lax.fori_loop(0, terms, note, (used, jnp.int32(0)), unroll=True)
        need.append(used > before)
    plan[0, used] = 0
    plan[1, used] = plan[1, jnp.maximum(used - 1, 0)]
    padded = 2 * ((used + 1) // 2)

    def tile_copy(kind):
        source = psi_ref if kind == 0 else got_ref.at[kind - 1]
        return pltpu.make_async_copy(source, tiles.at[kind], tile_sem.at[kind])

    def side_copies(n):
        term = plan[0, n]
        return (pltpu.make_async_copy(left_ref.at[term], lefts.at[n], left_sem.at[n]),
                pltpu.make_async_copy(right_ref.at[term], rights.at[n], right_sem.at[n]))

    for kind, wanted in enumerate(need):
        pl.when(wanted)(lambda kind=kind: tile_copy(kind).start())

    @pl.loop(0, padded)
    def _(n):
        for copy in side_copies(n):
            copy.start()

    start.wait()
    for kind, wanted in enumerate(need):
        pl.when(wanted)(lambda kind=kind: tile_copy(kind).wait())

    @pl.loop(0, padded // 2)
    def _(pair):
        spot = [2 * pair + t for t in range(2)]
        for n in spot:
            for copy in side_copies(n):
                copy.wait()
        kind = [plan[1, n] for n in spot]
        add_pair(
            [lambda s, k=k: tiles[k, pl.ds(s, 2)] for k in kind],
            [rights[n] for n in spot],
            [mpo_ref[plan[0, n]] for n in spot],
            [lefts[n] for n in spot],
            [(n < used).astype(jnp.float32) for n in spot],
            held, mixed, acc,
        )

    half = states // 2
    own_ref[...] = acc[pl.ds(core * half, half)]
    sent_ref[...] = acc[pl.ds((1 - core) * half, half)].astype(sent_ref.dtype)


def rest(term_class, psi, got, left, right, mpo, total, sectors):
    states, rows, width = psi.shape
    terms = left.shape[0]
    half = (states // 2, rows, width)
    return pl.pallas_call(
        functools.partial(rest_kernel, sectors),
        out_shape=(jax.ShapeDtypeStruct(half, jnp.float32), jax.ShapeDtypeStruct(half, jnp.bfloat16)),
        in_specs=[SMEM_SPEC, ANY_SPEC, ANY_SPEC, ANY_SPEC, ANY_SPEC, VMEM_SPEC, ANY_SPEC],
        out_specs=(VMEM_SPEC, VMEM_SPEC),
        scratch_shapes=[
            pltpu.VMEM((len(STEPS) + 1, states, rows, width), jnp.bfloat16),
            pltpu.VMEM((terms + 1, *left.shape[1:]), jnp.bfloat16),
            pltpu.VMEM((terms + 1, *right.shape[1:]), jnp.bfloat16),
            pltpu.VMEM((states, rows, width), jnp.float32),
            pltpu.VMEM((states, rows, 2 * width), jnp.bfloat16),
            pltpu.VMEM((2, states, rows, width), jnp.bfloat16),
            pltpu.SMEM((2, terms + 2), jnp.int32),
            pltpu.SemaphoreType.DMA((len(STEPS) + 1,)),
            pltpu.SemaphoreType.DMA((terms + 1,)),
            pltpu.SemaphoreType.DMA((terms + 1,)),
            pltpu.SemaphoreType.DMA(()),
        ],
        compiler_params=pltpu.CompilerParams(vmem_limit_bytes=VMEM_LIMIT),
        name="rest",
    )(term_class, psi, got, left, right, mpo, total)


def swap_kernel(sent_ref, inbox_ref, sems):
    group, sector, core = (lax.axis_index(name) for name in ("groups", "sector", "term"))
    sibling = (group, sector, 1 - core)
    barrier = pltpu.get_barrier_semaphore()
    pl.semaphore_signal(barrier, inc=1, device_id=sibling, device_id_type=MESH)
    pl.semaphore_wait(barrier, 1)
    copy = pltpu.make_async_remote_copy(
        src_ref=sent_ref, dst_ref=inbox_ref, send_sem=sems.at[0], recv_sem=sems.at[1],
        device_id=sibling, device_id_type=MESH,
    )
    copy.start()
    copy.wait()


def swapped(sent):
    return pl.pallas_call(
        swap_kernel,
        out_shape=jax.ShapeDtypeStruct(sent.shape, sent.dtype),
        in_specs=[ANY_SPEC],
        out_specs=ANY_SPEC,
        scratch_shapes=[pltpu.SemaphoreType.DMA((2,))],
        compiler_params=pltpu.CompilerParams(collective_id=1, has_side_effects=True, vmem_limit_bytes=VMEM_LIMIT),
        name="swap",
    )(sent)


def shards(psi_tiles, env_left, env_right, mpo_local, term_class):
    sectors = lax.axis_size("sector")
    psi, left, right = psi_tiles[0], env_left[0], env_right[0]
    got, total = front(term_class, psi, left, right, mpo_local, sectors)
    own, sent = rest(term_class, psi, got, left, right, mpo_local, total, sectors)
    return (own + swapped(sent).astype(jnp.float32)).astype(jnp.bfloat16)[None]


def solution(mesh):
    placed = (
        P(("groups", "sector"), None, None, None),
        P(("groups", "sector"), "term", None, None),
        P(("groups", "sector"), "term", None, None),
        P(("groups", "term"), None, None),
        P(("groups", "term")),
    )
    return jax.shard_map(
        shards,
        mesh=mesh,
        in_specs=placed,
        out_specs=P(("groups", "sector"), "term", None, None),
        check_vma=False,
    )
```

```python
import functools

import jax
import jax.numpy as jnp
from jax import lax
from jax.experimental import pallas as pl
from jax.experimental.pallas import tpu as pltpu
from jax.sharding import PartitionSpec as P

GRID = 4
MESH = pl.DeviceIdType.MESH
STEPS = (-1, 1, -GRID, GRID)
FRONT_KINDS, FRONT_SLOTS = 2, 8
VMEM_LIMIT = 56 * 1024 * 1024


def has_source(sector, sectors, step):
    column = lax.rem(sector + 1, GRID)
    if step == -1:
        return (sector >= 1) & (column > 0)
    if step == 1:
        return (sector + 1 < sectors) & (column < GRID - 1)
    if step < 0:
        return sector + step >= 0
    return sector + step < sectors


def add_pair(xs, rights, mpos, lefts, scales, held, mixed, acc):
    states, rows, width = acc.shape
    step = 16
    wide = states * step
    index = lambda axis: lax.broadcasted_iota(jnp.int32, (wide, wide), axis)
    same = lax.rem(index(0), step) == lax.rem(index(1), step)
    spread = (lax.broadcasted_iota(jnp.int32, (wide, states), 0) // step
              == lax.broadcasted_iota(jnp.int32, (wide, states), 1)).astype(jnp.bfloat16)
    spread_t = (lax.broadcasted_iota(jnp.int32, (states, wide), 1) // step
                == lax.broadcasted_iota(jnp.int32, (states, wide), 0)).astype(jnp.bfloat16)

    def dot(a, b):
        return jnp.dot(a, b, preferred_element_type=jnp.float32)

    krons = []
    for mpo, scale in zip(mpos, scales):
        tall = dot(spread, mpo).astype(jnp.bfloat16)
        krons.append(jnp.where(same, dot(tall, spread_t) * scale, 0.0).astype(jnp.bfloat16))
    zero = jnp.zeros((width, width), jnp.bfloat16)
    right = jnp.concatenate(
        [jnp.concatenate([rights[0], zero], 1), jnp.concatenate([zero, rights[1]], 1)], 0
    )
    for s in range(0, states, 2):
        x = jnp.concatenate([x(s).reshape(2 * rows, width) for x in xs], 1)
        held[pl.ds(s, 2)] = dot(x, right).astype(jnp.bfloat16).reshape(2, rows, 2 * width)
    for t in range(2):
        for r in range(0, rows, 2 * step):
            part = [
                held[:, pl.ds(r + o, step), pl.ds(t * width, width)].reshape(wide, width) for o in (0, step)
            ]
            out = dot(krons[t], jnp.concatenate(part, 1)).astype(jnp.bfloat16)
            for n, o in enumerate((0, step)):
                mixed[t, :, pl.ds(r + o, step), :] = out[:, n * width:(n + 1) * width].reshape(states, step, width)
    left = jnp.concatenate(lefts, 1)
    for s in range(0, states, 2):
        part = [jnp.concatenate([mixed[t, s], mixed[t, s + 1]], 1) for t in range(2)]
        out = dot(left, jnp.concatenate(part, 0))
        for n in range(2):
            acc[s + n] += out[:, n * width:(n + 1) * width]


def front_kernel(sectors, class_ref, psi_ref, left_ref, right_ref, mpo_ref, got_ref, acc,
                 tiles, lefts, rights, held, mixed, plan, send_sem, recv_sem, pass_sem, got_sem, local_sem):
    group, sector, core = (lax.axis_index(name) for name in ("groups", "sector", "term"))
    half = psi_ref.shape[0] // 2
    terms = left_ref.shape[0]
    mine = pl.ds(core * half, half)
    barrier = pltpu.get_barrier_semaphore()
    sibling = (group, sector, 1 - core)
    assert sectors % 2 == 0
    there = [has_source(sector, sectors, step) for step in STEPS]
    odd = lax.rem(sector, 2) == 1
    even = jnp.logical_not(odd)
    above, below = sector + 2 < sectors, sector >= 2
    partner = jnp.where(odd, sector - 1, sector + 1)
    near = jnp.where(odd, 0, 1)
    near_there = (odd & there[0]) | (even & there[1])
    up_out = above & ((sector + 4 < sectors) | (odd & there[1]))
    up_in = below & (above | (odd & has_source(sector - 2, sectors, 1)))
    down_out = below & ((sector >= 4) | (even & there[0]))
    down_in = above & (below | (even & has_source(sector + 2, sectors, -1)))
    across_0 = odd & below & has_source(sector - 1, sectors, -1)
    across_1 = even & above & has_source(sector + 1, sectors, 1)
    through = above & below

    def greet(target):
        pl.semaphore_signal(barrier, inc=1, device_id=target, device_id_type=MESH)

    greet(sibling)
    greet((group, partner, core))
    pl.when(above)(lambda: greet((group, sector + 2, core)))
    pl.when(below)(lambda: greet((group, sector - 2, core)))
    pl.semaphore_wait(barrier, 2 + above.astype(jnp.int32) + below.astype(jnp.int32))

    def send(source, slot, target):
        return pltpu.make_async_remote_copy(
            src_ref=source,
            dst_ref=got_ref.at[slot, mine],
            send_sem=send_sem.at[slot],
            recv_sem=recv_sem.at[slot],
            device_id=(group, target, core),
            device_id_type=MESH,
        )

    tile, lower, upper = psi_ref.at[mine], got_ref.at[4, mine], got_ref.at[5, mine]
    first = (
        (up_out, lambda: send(tile, 4, sector + 2)),
        (down_out, lambda: send(tile, 5, sector - 2)),
        (near_there, lambda: send(tile, 1 - near, partner)),
    )
    second = (
        (across_0, lambda: send(lower, 0, partner)),
        (through, lambda: send(lower, 2, sector + 2)),
        (across_1, lambda: send(upper, 1, partner)),
        (through, lambda: send(upper, 3, sector - 2)),
    )

    def passing(slot):
        return pltpu.make_async_remote_copy(
            src_ref=got_ref.at[slot, mine],
            dst_ref=got_ref.at[slot, mine],
            send_sem=pass_sem.at[slot],
            recv_sem=got_sem.at[slot],
            device_id=sibling,
            device_id_type=MESH,
        )

    def arrive(slot):
        send(tile, slot, partner).wait_recv()
        passing(slot).start()

    for live, copy in first:
        pl.when(live)(lambda copy=copy: copy().start())
    copies = [
        pltpu.make_async_copy(psi_ref, tiles.at[0], local_sem.at[0]),
        pltpu.make_async_copy(left_ref, lefts, local_sem.at[1]),
        pltpu.make_async_copy(right_ref, rights, local_sem.at[2]),
    ]
    for copy in copies:
        copy.start()

    def note(index, state):
        fresh = []
        for kind, (found, slots) in enumerate(state):
            match = class_ref[index] == (0 if kind == 0 else near + 1)
            slots = tuple(jnp.where(match & (found == n), index, slot) for n, slot in enumerate(slots))
            fresh.append((found + match.astype(jnp.int32), slots))
        return tuple(fresh)

    zero = jnp.int32(0)
    state = lax.fori_loop(0, terms, note, tuple((zero, (zero,) * FRONT_SLOTS) for _ in range(FRONT_KINDS)))
    for kind, (found, slots) in enumerate(state):
        for n, slot in enumerate(slots):
            plan[0, kind * FRONT_SLOTS + n] = slot
            plan[1, kind * FRONT_SLOTS + n] = (n < found).astype(jnp.int32)
    acc[...] = jnp.zeros_like(acc)
    for copy in copies:
        copy.wait()

    @pl.loop(0, FRONT_KINDS)
    def _(phase):
        @pl.when(phase == 1)
        def _():
            @pl.when(up_in)
            def _():
                send(tile, 4, partner).wait_recv()
                for live, copy in second[:2]:
                    pl.when(live)(lambda copy=copy: copy().start())

            @pl.when(down_in)
            def _():
                send(tile, 5, partner).wait_recv()
                for live, copy in second[2:]:
                    pl.when(live)(lambda copy=copy: copy().start())

            @pl.when(near_there)
            def _():
                arrive(near)
                passing(near).wait()
                copy = pltpu.make_async_copy(got_ref.at[near], tiles.at[1], local_sem.at[3])
                copy.start()
                copy.wait()

        live = (phase == 0) | near_there

        @pl.when(live)
        def _():
            @pl.loop(0, FRONT_SLOTS // 2)
            def _(pair):
                spot = [phase * FRONT_SLOTS + 2 * pair + t for t in range(2)]
                term = [plan[0, n] for n in spot]
                add_pair(
                    [lambda s: tiles[phase, pl.ds(s, 2)]] * 2,
                    [rights[i] for i in term],
                    [mpo_ref[i] for i in term],
                    [lefts[i] for i in term],
                    [plan[1, n].astype(jnp.float32) for n in spot],
                    held, mixed, acc,
                )

    late = ((odd & there[1]) | (even & there[0]), 1 - near), (there[2], 2), (there[3], 3)
    for live, slot in late:
        pl.when(live)(lambda slot=slot: arrive(slot))
    for live, slot in late:
        pl.when(live)(lambda slot=slot: passing(slot).wait())
    for live, copy in first + second:
        pl.when(live)(lambda copy=copy: copy().wait_send())


SMEM_SPEC = pl.BlockSpec(memory_space=pltpu.SMEM)
VMEM_SPEC = pl.BlockSpec(memory_space=pltpu.VMEM)
ANY_SPEC = pl.BlockSpec(memory_space=pl.ANY)


def front(term_class, psi, left, right, mpo, sectors):
    states, rows, width = psi.shape
    slots = len(STEPS)
    return pl.pallas_call(
        functools.partial(front_kernel, sectors),
        out_shape=(
            jax.ShapeDtypeStruct((slots + 2, *psi.shape), psi.dtype),
            jax.ShapeDtypeStruct(psi.shape, jnp.float32),
        ),
        in_specs=[SMEM_SPEC, ANY_SPEC, ANY_SPEC, ANY_SPEC, VMEM_SPEC],
        out_specs=(ANY_SPEC, VMEM_SPEC),
        scratch_shapes=[
            pltpu.VMEM((FRONT_KINDS, states, rows, width), jnp.bfloat16),
            pltpu.VMEM(left.shape, jnp.bfloat16),
            pltpu.VMEM(right.shape, jnp.bfloat16),
            pltpu.VMEM((states, rows, 2 * width), jnp.bfloat16),
            pltpu.VMEM((2, states, rows, width), jnp.bfloat16),
            pltpu.SMEM((2, FRONT_KINDS * FRONT_SLOTS), jnp.int32),
        ] + [pltpu.SemaphoreType.DMA((slots + 2,))] * 5,
        compiler_params=pltpu.CompilerParams(collective_id=0, has_side_effects=True, vmem_limit_bytes=VMEM_LIMIT),
        name="front",
    )(term_class, psi, left, right, mpo)


def rest_kernel(sectors, class_ref, psi_ref, got_ref, left_ref, right_ref, mpo_ref, total_ref, own_ref, sent_ref,
                tiles, lefts, rights, acc, held, mixed, plan, tile_sem, left_sem, right_sem, acc_sem):
    sector, core = lax.axis_index("sector"), lax.axis_index("term")
    terms = left_ref.shape[0]
    states = acc.shape[0]
    start = pltpu.make_async_copy(total_ref, acc, acc_sem)
    start.start()
    near = 2 - lax.rem(sector, 2)
    used = jnp.int32(0)
    need = []
    for kind in range(len(STEPS) + 1):
        there = jnp.bool_(True) if kind == 0 else has_source(sector, sectors, STEPS[kind - 1])
        skip = FRONT_SLOTS if kind == 0 else jnp.where(near == kind, FRONT_SLOTS, 0)
        before = used

        def note(index, state, kind=kind, there=there, skip=skip):
            used, found = state
            match = (class_ref[index] == kind) & there
            plan[0, used] = index
            plan[1, used] = kind
            take = match & (found >= skip)
            return used + take.astype(jnp.int32), found + match.astype(jnp.int32)

        used, found = lax.fori_loop(0, terms, note, (used, jnp.int32(0)), unroll=True)
        need.append(used > before)
    plan[0, used] = 0
    plan[1, used] = plan[1, jnp.maximum(used - 1, 0)]
    padded = 2 * ((used + 1) // 2)

    def tile_copy(kind):
        source = psi_ref if kind == 0 else got_ref.at[kind - 1]
        return pltpu.make_async_copy(source, tiles.at[kind], tile_sem.at[kind])

    def side_copies(n):
        term = plan[0, n]
        return (pltpu.make_async_copy(left_ref.at[term], lefts.at[n], left_sem.at[n]),
                pltpu.make_async_copy(right_ref.at[term], rights.at[n], right_sem.at[n]))

    for kind, wanted in enumerate(need):
        pl.when(wanted)(lambda kind=kind: tile_copy(kind).start())

    @pl.loop(0, padded)
    def _(n):
        for copy in side_copies(n):
            copy.start()

    start.wait()
    for kind, wanted in enumerate(need):
        pl.when(wanted)(lambda kind=kind: tile_copy(kind).wait())

    @pl.loop(0, padded // 2)
    def _(pair):
        spot = [2 * pair + t for t in range(2)]
        for n in spot:
            for copy in side_copies(n):
                copy.wait()
        kind = [plan[1, n] for n in spot]
        add_pair(
            [lambda s, k=k: tiles[k, pl.ds(s, 2)] for k in kind],
            [rights[n] for n in spot],
            [mpo_ref[plan[0, n]] for n in spot],
            [lefts[n] for n in spot],
            [(n < used).astype(jnp.float32) for n in spot],
            held, mixed, acc,
        )

    half = states // 2
    own_ref[...] = acc[pl.ds(core * half, half)]
    sent_ref[...] = acc[pl.ds((1 - core) * half, half)].astype(sent_ref.dtype)


def rest(term_class, psi, got, left, right, mpo, total, sectors):
    states, rows, width = psi.shape
    terms = left.shape[0]
    half = (states // 2, rows, width)
    return pl.pallas_call(
        functools.partial(rest_kernel, sectors),
        out_shape=(jax.ShapeDtypeStruct(half, jnp.float32), jax.ShapeDtypeStruct(half, jnp.bfloat16)),
        in_specs=[SMEM_SPEC, ANY_SPEC, ANY_SPEC, ANY_SPEC, ANY_SPEC, VMEM_SPEC, ANY_SPEC],
        out_specs=(VMEM_SPEC, VMEM_SPEC),
        scratch_shapes=[
            pltpu.VMEM((len(STEPS) + 1, states, rows, width), jnp.bfloat16),
            pltpu.VMEM((terms + 1, *left.shape[1:]), jnp.bfloat16),
            pltpu.VMEM((terms + 1, *right.shape[1:]), jnp.bfloat16),
            pltpu.VMEM((states, rows, width), jnp.float32),
            pltpu.VMEM((states, rows, 2 * width), jnp.bfloat16),
            pltpu.VMEM((2, states, rows, width), jnp.bfloat16),
            pltpu.SMEM((2, terms + 2), jnp.int32),
            pltpu.SemaphoreType.DMA((len(STEPS) + 1,)),
            pltpu.SemaphoreType.DMA((terms + 1,)),
            pltpu.SemaphoreType.DMA((terms + 1,)),
            pltpu.SemaphoreType.DMA(()),
        ],
        compiler_params=pltpu.CompilerParams(vmem_limit_bytes=VMEM_LIMIT),
        name="rest",
    )(term_class, psi, got, left, right, mpo, total)


def swap_kernel(sent_ref, inbox_ref, sems):
    group, sector, core = (lax.axis_index(name) for name in ("groups", "sector", "term"))
    sibling = (group, sector, 1 - core)
    barrier = pltpu.get_barrier_semaphore()
    pl.semaphore_signal(barrier, inc=1, device_id=sibling, device_id_type=MESH)
    pl.semaphore_wait(barrier, 1)
    copy = pltpu.make_async_remote_copy(
        src_ref=sent_ref, dst_ref=inbox_ref, send_sem=sems.at[0], recv_sem=sems.at[1],
        device_id=sibling, device_id_type=MESH,
    )
    copy.start()
    copy.wait()


def swapped(sent):
    return pl.pallas_call(
        swap_kernel,
        out_shape=jax.ShapeDtypeStruct(sent.shape, sent.dtype),
        in_specs=[ANY_SPEC],
        out_specs=ANY_SPEC,
        scratch_shapes=[pltpu.SemaphoreType.DMA((2,))],
        compiler_params=pltpu.CompilerParams(collective_id=1, has_side_effects=True, vmem_limit_bytes=VMEM_LIMIT),
        name="swap",
    )(sent)


def shards(psi_tiles, env_left, env_right, mpo_local, term_class):
    sectors = lax.axis_size("sector")
    psi, left, right = psi_tiles[0], env_left[0], env_right[0]
    got, total = front(term_class, psi, left, right, mpo_local, sectors)
    own, sent = rest(term_class, psi, got, left, right, mpo_local, total, sectors)
    return (own + swapped(sent).astype(jnp.float32)).astype(jnp.bfloat16)[None]


def solution(mesh):
    placed = (
        P(("groups", "sector"), None, None, None),
        P(("groups", "sector"), "term", None, None),
        P(("groups", "sector"), "term", None, None),
        P(("groups", "term"), None, None),
        P(("groups", "term")),
    )
    return jax.shard_map(
        shards,
        mesh=mesh,
        in_specs=placed,
        out_specs=P(("groups", "sector"), "term", None, None),
        check_vma=False,
    )
```

```python
import functools

import jax
import jax.numpy as jnp
from jax import lax
from jax.experimental import pallas as pl
from jax.experimental.pallas import tpu as pltpu
from jax.sharding import PartitionSpec as P

GRID = 4
MESH = pl.DeviceIdType.MESH
STEPS = (-1, 1, -GRID, GRID)
FRONT_KINDS, FRONT_SLOTS = 2, 8
VMEM_LIMIT = 56 * 1024 * 1024


def has_source(sector, sectors, step):
    column = lax.rem(sector + 1, GRID)
    if step == -1:
        return (sector >= 1) & (column > 0)
    if step == 1:
        return (sector + 1 < sectors) & (column < GRID - 1)
    if step < 0:
        return sector + step >= 0
    return sector + step < sectors


def add_pair(xs, rights, mpo_ref, terms, lefts, scales, held, mixed, acc):
    states, rows, width = acc.shape
    step = 16
    wide = states * step
    index = lambda axis: lax.broadcasted_iota(jnp.int32, (wide, wide), axis)
    same = lax.rem(index(0), step) == lax.rem(index(1), step)
    entry = lambda axis: lax.broadcasted_iota(jnp.int32, (states * states, wide), axis)
    column = lax.rem(entry(0), states) == entry(1) // step
    spread = (lax.broadcasted_iota(jnp.int32, (wide, states * states), 0) // step
              == lax.broadcasted_iota(jnp.int32, (wide, states * states), 1) // states).astype(jnp.bfloat16)
    flat = mpo_ref[...].reshape(states * states, mpo_ref.shape[2]).astype(jnp.float32)
    number = lax.broadcasted_iota(jnp.int32, flat.shape, 1)

    def dot(a, b):
        return jnp.dot(a, b, preferred_element_type=jnp.float32)

    krons = []
    for term, scale in zip(terms, scales):
        values = jnp.sum(jnp.where(number == term, flat, 0.0), 1, keepdims=True) * scale
        wide_rows = jnp.where(column, values, 0.0).astype(jnp.bfloat16)
        krons.append(jnp.where(same, dot(spread, wide_rows), 0.0).astype(jnp.bfloat16))
    zero = jnp.zeros((width, width), jnp.bfloat16)
    right = jnp.concatenate(
        [jnp.concatenate([rights[0], zero], 1), jnp.concatenate([zero, rights[1]], 1)], 0
    )
    for s in range(0, states, 2):
        x = jnp.concatenate([x(s).reshape(2 * rows, width) for x in xs], 1)
        held[pl.ds(s, 2)] = dot(x, right).astype(jnp.bfloat16).reshape(2, rows, 2 * width)
    for t in range(2):
        for r in range(0, rows, 2 * step):
            part = [
                held[:, pl.ds(r + o, step), pl.ds(t * width, width)].reshape(wide, width) for o in (0, step)
            ]
            out = dot(krons[t], jnp.concatenate(part, 1)).astype(jnp.bfloat16)
            for n, o in enumerate((0, step)):
                mixed[t, :, pl.ds(r + o, step), :] = out[:, n * width:(n + 1) * width].reshape(states, step, width)
    left = jnp.concatenate(lefts, 1)
    for s in range(0, states, 2):
        part = [jnp.concatenate([mixed[t, s], mixed[t, s + 1]], 1) for t in range(2)]
        out = dot(left, jnp.concatenate(part, 0))
        for n in range(2):
            acc[s + n] += out[:, n * width:(n + 1) * width]


def front_kernel(sectors, class_ref, psi_ref, left_ref, right_ref, mpo_ref, got_ref, acc,
                 tiles, lefts, rights, held, mixed, plan, send_sem, recv_sem, pass_sem, got_sem, local_sem):
    group, sector, core = (lax.axis_index(name) for name in ("groups", "sector", "term"))
    half = psi_ref.shape[0] // 2
    terms = left_ref.shape[0]
    mine = pl.ds(core * half, half)
    barrier = pltpu.get_barrier_semaphore()
    sibling = (group, sector, 1 - core)
    assert sectors % 2 == 0
    there = [has_source(sector, sectors, step) for step in STEPS]
    odd = lax.rem(sector, 2) == 1
    even = jnp.logical_not(odd)
    above, below = sector + 2 < sectors, sector >= 2
    partner = jnp.where(odd, sector - 1, sector + 1)
    near = jnp.where(odd, 0, 1)
    near_there = (odd & there[0]) | (even & there[1])
    up_out = above & ((sector + 4 < sectors) | (odd & there[1]))
    up_in = below & (above | (odd & has_source(sector - 2, sectors, 1)))
    down_out = below & ((sector >= 4) | (even & there[0]))
    down_in = above & (below | (even & has_source(sector + 2, sectors, -1)))
    across_0 = odd & below & has_source(sector - 1, sectors, -1)
    across_1 = even & above & has_source(sector + 1, sectors, 1)
    through = above & below

    def greet(target):
        pl.semaphore_signal(barrier, inc=1, device_id=target, device_id_type=MESH)

    greet(sibling)
    greet((group, partner, core))
    pl.when(above)(lambda: greet((group, sector + 2, core)))
    pl.when(below)(lambda: greet((group, sector - 2, core)))
    pl.semaphore_wait(barrier, 2 + above.astype(jnp.int32) + below.astype(jnp.int32))

    def send(source, slot, target):
        return pltpu.make_async_remote_copy(
            src_ref=source,
            dst_ref=got_ref.at[slot, mine],
            send_sem=send_sem.at[slot],
            recv_sem=recv_sem.at[slot],
            device_id=(group, target, core),
            device_id_type=MESH,
        )

    tile, lower, upper = psi_ref.at[mine], got_ref.at[4, mine], got_ref.at[5, mine]
    first = (
        (up_out, lambda: send(tile, 4, sector + 2)),
        (down_out, lambda: send(tile, 5, sector - 2)),
        (near_there, lambda: send(tile, 1 - near, partner)),
    )
    second = (
        (across_0, lambda: send(lower, 0, partner)),
        (through, lambda: send(lower, 2, sector + 2)),
        (across_1, lambda: send(upper, 1, partner)),
        (through, lambda: send(upper, 3, sector - 2)),
    )

    def passing(slot):
        return pltpu.make_async_remote_copy(
            src_ref=got_ref.at[slot, mine],
            dst_ref=got_ref.at[slot, mine],
            send_sem=pass_sem.at[slot],
            recv_sem=got_sem.at[slot],
            device_id=sibling,
            device_id_type=MESH,
        )

    def arrive(slot):
        send(tile, slot, partner).wait_recv()
        passing(slot).start()

    for live, copy in first:
        pl.when(live)(lambda copy=copy: copy().start())
    copies = [
        pltpu.make_async_copy(psi_ref, tiles.at[0], local_sem.at[0]),
        pltpu.make_async_copy(left_ref, lefts, local_sem.at[1]),
        pltpu.make_async_copy(right_ref, rights, local_sem.at[2]),
    ]
    for copy in copies:
        copy.start()

    def note(index, state):
        fresh = []
        for kind, (found, slots) in enumerate(state):
            match = class_ref[index] == (0 if kind == 0 else near + 1)
            slots = tuple(jnp.where(match & (found == n), index, slot) for n, slot in enumerate(slots))
            fresh.append((found + match.astype(jnp.int32), slots))
        return tuple(fresh)

    zero = jnp.int32(0)
    state = lax.fori_loop(0, terms, note, tuple((zero, (zero,) * FRONT_SLOTS) for _ in range(FRONT_KINDS)))
    for kind, (found, slots) in enumerate(state):
        for n, slot in enumerate(slots):
            plan[0, kind * FRONT_SLOTS + n] = slot
            plan[1, kind * FRONT_SLOTS + n] = (n < found).astype(jnp.int32)
    acc[...] = jnp.zeros_like(acc)
    for copy in copies:
        copy.wait()

    @pl.loop(0, FRONT_KINDS)
    def _(phase):
        @pl.when(phase == 1)
        def _():
            @pl.when(up_in)
            def _():
                send(tile, 4, partner).wait_recv()
                for live, copy in second[:2]:
                    pl.when(live)(lambda copy=copy: copy().start())

            @pl.when(down_in)
            def _():
                send(tile, 5, partner).wait_recv()
                for live, copy in second[2:]:
                    pl.when(live)(lambda copy=copy: copy().start())

            @pl.when(near_there)
            def _():
                arrive(near)
                passing(near).wait()
                copy = pltpu.make_async_copy(got_ref.at[near], tiles.at[1], local_sem.at[3])
                copy.start()
                copy.wait()

        live = (phase == 0) | near_there

        @pl.when(live)
        def _():
            @pl.loop(0, FRONT_SLOTS // 2)
            def _(pair):
                spot = [phase * FRONT_SLOTS + 2 * pair + t for t in range(2)]
                term = [plan[0, n] for n in spot]
                add_pair(
                    [lambda s: tiles[phase, pl.ds(s, 2)]] * 2,
                    [rights[i] for i in term],
                    mpo_ref, term,
                    [lefts[i] for i in term],
                    [plan[1, n].astype(jnp.float32) for n in spot],
                    held, mixed, acc,
                )

    late = ((odd & there[1]) | (even & there[0]), 1 - near), (there[2], 2), (there[3], 3)
    for live, slot in late:
        pl.when(live)(lambda slot=slot: arrive(slot))
    for live, slot in late:
        pl.when(live)(lambda slot=slot: passing(slot).wait())
    for live, copy in first + second:
        pl.when(live)(lambda copy=copy: copy().wait_send())


SMEM_SPEC = pl.BlockSpec(memory_space=pltpu.SMEM)
VMEM_SPEC = pl.BlockSpec(memory_space=pltpu.VMEM)
ANY_SPEC = pl.BlockSpec(memory_space=pl.ANY)


def front(term_class, psi, left, right, mpo, sectors):
    states, rows, width = psi.shape
    slots = len(STEPS)
    return pl.pallas_call(
        functools.partial(front_kernel, sectors),
        out_shape=(
            jax.ShapeDtypeStruct((slots + 2, *psi.shape), psi.dtype),
            jax.ShapeDtypeStruct(psi.shape, jnp.float32),
        ),
        in_specs=[SMEM_SPEC, ANY_SPEC, ANY_SPEC, ANY_SPEC, VMEM_SPEC],
        out_specs=(ANY_SPEC, VMEM_SPEC),
        scratch_shapes=[
            pltpu.VMEM((FRONT_KINDS, states, rows, width), jnp.bfloat16),
            pltpu.VMEM(left.shape, jnp.bfloat16),
            pltpu.VMEM(right.shape, jnp.bfloat16),
            pltpu.VMEM((states, rows, 2 * width), jnp.bfloat16),
            pltpu.VMEM((2, states, rows, width), jnp.bfloat16),
            pltpu.SMEM((2, FRONT_KINDS * FRONT_SLOTS), jnp.int32),
        ] + [pltpu.SemaphoreType.DMA((slots + 2,))] * 5,
        compiler_params=pltpu.CompilerParams(collective_id=0, has_side_effects=True, vmem_limit_bytes=VMEM_LIMIT),
        name="front",
    )(term_class, psi, left, right, mpo)


def rest_kernel(sectors, class_ref, psi_ref, got_ref, left_ref, right_ref, mpo_ref, total_ref, own_ref, sent_ref,
                tiles, lefts, rights, acc, held, mixed, plan, tile_sem, left_sem, right_sem, acc_sem):
    sector, core = lax.axis_index("sector"), lax.axis_index("term")
    terms = left_ref.shape[0]
    states = acc.shape[0]
    start = pltpu.make_async_copy(total_ref, acc, acc_sem)
    start.start()
    near = 2 - lax.rem(sector, 2)
    used = jnp.int32(0)
    need = []
    for kind in range(len(STEPS) + 1):
        there = jnp.bool_(True) if kind == 0 else has_source(sector, sectors, STEPS[kind - 1])
        skip = FRONT_SLOTS if kind == 0 else jnp.where(near == kind, FRONT_SLOTS, 0)
        before = used

        def note(index, state, kind=kind, there=there, skip=skip):
            used, found = state
            match = (class_ref[index] == kind) & there
            plan[0, used] = index
            plan[1, used] = kind
            take = match & (found >= skip)
            return used + take.astype(jnp.int32), found + match.astype(jnp.int32)

        used, found = lax.fori_loop(0, terms, note, (used, jnp.int32(0)), unroll=True)
        need.append(used > before)
    plan[0, used] = 0
    plan[1, used] = plan[1, jnp.maximum(used - 1, 0)]
    padded = 2 * ((used + 1) // 2)

    def tile_copy(kind):
        source = psi_ref if kind == 0 else got_ref.at[kind - 1]
        return pltpu.make_async_copy(source, tiles.at[kind], tile_sem.at[kind])

    def side_copies(n):
        term = plan[0, n]
        return (pltpu.make_async_copy(left_ref.at[term], lefts.at[n], left_sem.at[n]),
                pltpu.make_async_copy(right_ref.at[term], rights.at[n], right_sem.at[n]))

    for kind, wanted in enumerate(need):
        pl.when(wanted)(lambda kind=kind: tile_copy(kind).start())

    @pl.loop(0, padded)
    def _(n):
        for copy in side_copies(n):
            copy.start()

    start.wait()
    for kind, wanted in enumerate(need):
        pl.when(wanted)(lambda kind=kind: tile_copy(kind).wait())

    @pl.loop(0, padded // 2)
    def _(pair):
        spot = [2 * pair + t for t in range(2)]
        for n in spot:
            for copy in side_copies(n):
                copy.wait()
        kind = [plan[1, n] for n in spot]
        add_pair(
            [lambda s, k=k: tiles[k, pl.ds(s, 2)] for k in kind],
            [rights[n] for n in spot],
            mpo_ref, [plan[0, n] for n in spot],
            [lefts[n] for n in spot],
            [(n < used).astype(jnp.float32) for n in spot],
            held, mixed, acc,
        )

    half = states // 2
    own_ref[...] = acc[pl.ds(core * half, half)]
    sent_ref[...] = acc[pl.ds((1 - core) * half, half)].astype(sent_ref.dtype)


def rest(term_class, psi, got, left, right, mpo, total, sectors):
    states, rows, width = psi.shape
    terms = left.shape[0]
    half = (states // 2, rows, width)
    return pl.pallas_call(
        functools.partial(rest_kernel, sectors),
        out_shape=(jax.ShapeDtypeStruct(half, jnp.float32), jax.ShapeDtypeStruct(half, jnp.bfloat16)),
        in_specs=[SMEM_SPEC, ANY_SPEC, ANY_SPEC, ANY_SPEC, ANY_SPEC, VMEM_SPEC, ANY_SPEC],
        out_specs=(VMEM_SPEC, VMEM_SPEC),
        scratch_shapes=[
            pltpu.VMEM((len(STEPS) + 1, states, rows, width), jnp.bfloat16),
            pltpu.VMEM((terms + 1, *left.shape[1:]), jnp.bfloat16),
            pltpu.VMEM((terms + 1, *right.shape[1:]), jnp.bfloat16),
            pltpu.VMEM((states, rows, width), jnp.float32),
            pltpu.VMEM((states, rows, 2 * width), jnp.bfloat16),
            pltpu.VMEM((2, states, rows, width), jnp.bfloat16),
            pltpu.SMEM((2, terms + 2), jnp.int32),
            pltpu.SemaphoreType.DMA((len(STEPS) + 1,)),
            pltpu.SemaphoreType.DMA((terms + 1,)),
            pltpu.SemaphoreType.DMA((terms + 1,)),
            pltpu.SemaphoreType.DMA(()),
        ],
        compiler_params=pltpu.CompilerParams(vmem_limit_bytes=VMEM_LIMIT),
        name="rest",
    )(term_class, psi, got, left, right, mpo, total)


def swap_kernel(sent_ref, inbox_ref, sems):
    group, sector, core = (lax.axis_index(name) for name in ("groups", "sector", "term"))
    sibling = (group, sector, 1 - core)
    barrier = pltpu.get_barrier_semaphore()
    pl.semaphore_signal(barrier, inc=1, device_id=sibling, device_id_type=MESH)
    pl.semaphore_wait(barrier, 1)
    copy = pltpu.make_async_remote_copy(
        src_ref=sent_ref, dst_ref=inbox_ref, send_sem=sems.at[0], recv_sem=sems.at[1],
        device_id=sibling, device_id_type=MESH,
    )
    copy.start()
    copy.wait()


def swapped(sent):
    return pl.pallas_call(
        swap_kernel,
        out_shape=jax.ShapeDtypeStruct(sent.shape, sent.dtype),
        in_specs=[ANY_SPEC],
        out_specs=ANY_SPEC,
        scratch_shapes=[pltpu.SemaphoreType.DMA((2,))],
        compiler_params=pltpu.CompilerParams(collective_id=1, has_side_effects=True, vmem_limit_bytes=VMEM_LIMIT),
        name="swap",
    )(sent)


def shards(psi_tiles, env_left, env_right, mpo_local, term_class):
    sectors = lax.axis_size("sector")
    psi, left, right = psi_tiles[0], env_left[0], env_right[0]
    mpo = jnp.transpose(mpo_local, (1, 2, 0))
    got, total = front(term_class, psi, left, right, mpo, sectors)
    own, sent = rest(term_class, psi, got, left, right, mpo, total, sectors)
    return (own + swapped(sent).astype(jnp.float32)).astype(jnp.bfloat16)[None]


def solution(mesh):
    placed = (
        P(("groups", "sector"), None, None, None),
        P(("groups", "sector"), "term", None, None),
        P(("groups", "sector"), "term", None, None),
        P(("groups", "term"), None, None),
        P(("groups", "term")),
    )
    return jax.shard_map(
        shards,
        mesh=mesh,
        in_specs=placed,
        out_specs=P(("groups", "sector"), "term", None, None),
        check_vma=False,
    )
```

```python
import functools

import jax
import jax.numpy as jnp
from jax import lax
from jax.experimental import pallas as pl
from jax.experimental.pallas import tpu as pltpu
from jax.sharding import PartitionSpec as P

GRID = 4
MESH = pl.DeviceIdType.MESH
STEPS = (-1, 1, -GRID, GRID)
FRONT_KINDS, FRONT_SLOTS = 2, 8
VMEM_LIMIT = 56 * 1024 * 1024


def has_source(sector, sectors, step):
    column = lax.rem(sector + 1, GRID)
    if step == -1:
        return (sector >= 1) & (column > 0)
    if step == 1:
        return (sector + 1 < sectors) & (column < GRID - 1)
    if step < 0:
        return sector + step >= 0
    return sector + step < sectors


def add_pair(xs, rights, mpo_ref, terms, lefts, scales, held, mixed, acc, before_sum=lambda: None):
    states, rows, width = acc.shape
    step = 16
    wide = states * step
    index = lambda axis: lax.broadcasted_iota(jnp.int32, (wide, wide), axis)
    same = lax.rem(index(0), step) == lax.rem(index(1), step)
    entry = lambda axis: lax.broadcasted_iota(jnp.int32, (states * states, wide), axis)
    column = lax.rem(entry(0), states) == entry(1) // step
    spread = (lax.broadcasted_iota(jnp.int32, (wide, states * states), 0) // step
              == lax.broadcasted_iota(jnp.int32, (wide, states * states), 1) // states).astype(jnp.bfloat16)
    flat = mpo_ref[...].reshape(states * states, mpo_ref.shape[2]).astype(jnp.float32)
    number = lax.broadcasted_iota(jnp.int32, flat.shape, 1)

    def dot(a, b):
        return jnp.dot(a, b, preferred_element_type=jnp.float32)

    krons = []
    for term, scale in zip(terms, scales):
        values = jnp.sum(jnp.where(number == term, flat, 0.0), 1, keepdims=True) * scale
        wide_rows = jnp.where(column, values, 0.0).astype(jnp.bfloat16)
        krons.append(jnp.where(same, dot(spread, wide_rows), 0.0).astype(jnp.bfloat16))
    zero = jnp.zeros((width, width), jnp.bfloat16)
    right = jnp.concatenate(
        [jnp.concatenate([rights[0], zero], 1), jnp.concatenate([zero, rights[1]], 1)], 0
    )
    for s in range(0, states, 2):
        x = jnp.concatenate([x(s).reshape(2 * rows, width) for x in xs], 1)
        held[pl.ds(s, 2)] = dot(x, right).astype(jnp.bfloat16).reshape(2, rows, 2 * width)
    for t in range(2):
        for r in range(0, rows, 2 * step):
            part = [
                held[:, pl.ds(r + o, step), pl.ds(t * width, width)].reshape(wide, width) for o in (0, step)
            ]
            out = dot(krons[t], jnp.concatenate(part, 1)).astype(jnp.bfloat16)
            for n, o in enumerate((0, step)):
                mixed[t, :, pl.ds(r + o, step), :] = out[:, n * width:(n + 1) * width].reshape(states, step, width)
    before_sum()
    left = jnp.concatenate(lefts, 1)
    for s in range(0, states, 2):
        part = [jnp.concatenate([mixed[t, s], mixed[t, s + 1]], 1) for t in range(2)]
        out = dot(left, jnp.concatenate(part, 0))
        for n in range(2):
            acc[s + n] += out[:, n * width:(n + 1) * width]


def front_kernel(sectors, class_ref, psi_ref, left_ref, right_ref, mpo_ref, got_ref, acc,
                 tiles, lefts, rights, held, mixed, plan, send_sem, recv_sem, pass_sem, got_sem, local_sem):
    group, sector, core = (lax.axis_index(name) for name in ("groups", "sector", "term"))
    half = psi_ref.shape[0] // 2
    terms = left_ref.shape[0]
    mine = pl.ds(core * half, half)
    barrier = pltpu.get_barrier_semaphore()
    sibling = (group, sector, 1 - core)
    assert sectors % 2 == 0
    there = [has_source(sector, sectors, step) for step in STEPS]
    odd = lax.rem(sector, 2) == 1
    even = jnp.logical_not(odd)
    above, below = sector + 2 < sectors, sector >= 2
    partner = jnp.where(odd, sector - 1, sector + 1)
    near = jnp.where(odd, 0, 1)
    near_there = (odd & there[0]) | (even & there[1])
    up_out = above & ((sector + 4 < sectors) | (odd & there[1]))
    up_in = below & (above | (odd & has_source(sector - 2, sectors, 1)))
    down_out = below & ((sector >= 4) | (even & there[0]))
    down_in = above & (below | (even & has_source(sector + 2, sectors, -1)))
    across_0 = odd & below & has_source(sector - 1, sectors, -1)
    across_1 = even & above & has_source(sector + 1, sectors, 1)
    through = above & below

    def greet(target):
        pl.semaphore_signal(barrier, inc=1, device_id=target, device_id_type=MESH)

    greet(sibling)
    greet((group, partner, core))
    pl.when(above)(lambda: greet((group, sector + 2, core)))
    pl.when(below)(lambda: greet((group, sector - 2, core)))
    pl.semaphore_wait(barrier, 2 + above.astype(jnp.int32) + below.astype(jnp.int32))

    def send(source, slot, target):
        return pltpu.make_async_remote_copy(
            src_ref=source,
            dst_ref=got_ref.at[slot, mine],
            send_sem=send_sem.at[slot],
            recv_sem=recv_sem.at[slot],
            device_id=(group, target, core),
            device_id_type=MESH,
        )

    tile, lower, upper = psi_ref.at[mine], got_ref.at[4, mine], got_ref.at[5, mine]
    first = (
        (up_out, lambda: send(tile, 4, sector + 2)),
        (down_out, lambda: send(tile, 5, sector - 2)),
        (near_there, lambda: send(tile, 1 - near, partner)),
    )
    second = (
        (across_0, lambda: send(lower, 0, partner)),
        (through, lambda: send(lower, 2, sector + 2)),
        (across_1, lambda: send(upper, 1, partner)),
        (through, lambda: send(upper, 3, sector - 2)),
    )

    def passing(slot):
        return pltpu.make_async_remote_copy(
            src_ref=got_ref.at[slot, mine],
            dst_ref=got_ref.at[slot, mine],
            send_sem=pass_sem.at[slot],
            recv_sem=got_sem.at[slot],
            device_id=sibling,
            device_id_type=MESH,
        )

    def arrive(slot):
        send(tile, slot, partner).wait_recv()
        passing(slot).start()

    for live, copy in first:
        pl.when(live)(lambda copy=copy: copy().start())
    copies = [
        pltpu.make_async_copy(psi_ref, tiles.at[0], local_sem.at[0]),
        pltpu.make_async_copy(left_ref, lefts, local_sem.at[1]),
        pltpu.make_async_copy(right_ref, rights, local_sem.at[2]),
    ]
    for copy in copies:
        copy.start()

    def note(index, state):
        fresh = []
        for kind, (found, slots) in enumerate(state):
            match = class_ref[index] == (0 if kind == 0 else near + 1)
            slots = tuple(jnp.where(match & (found == n), index, slot) for n, slot in enumerate(slots))
            fresh.append((found + match.astype(jnp.int32), slots))
        return tuple(fresh)

    zero = jnp.int32(0)
    state = lax.fori_loop(0, terms, note, tuple((zero, (zero,) * FRONT_SLOTS) for _ in range(FRONT_KINDS)))
    for kind, (found, slots) in enumerate(state):
        for n, slot in enumerate(slots):
            plan[0, kind * FRONT_SLOTS + n] = slot
            plan[1, kind * FRONT_SLOTS + n] = (n < found).astype(jnp.int32)
    acc[...] = jnp.zeros_like(acc)
    for copy in copies:
        copy.wait()

    @pl.loop(0, FRONT_KINDS)
    def _(phase):
        @pl.when(phase == 1)
        def _():
            @pl.when(up_in)
            def _():
                send(tile, 4, partner).wait_recv()
                for live, copy in second[:2]:
                    pl.when(live)(lambda copy=copy: copy().start())

            @pl.when(down_in)
            def _():
                send(tile, 5, partner).wait_recv()
                for live, copy in second[2:]:
                    pl.when(live)(lambda copy=copy: copy().start())

            @pl.when(near_there)
            def _():
                arrive(near)
                passing(near).wait()
                copy = pltpu.make_async_copy(got_ref.at[near], tiles.at[1], local_sem.at[3])
                copy.start()
                copy.wait()

        live = (phase == 0) | near_there

        @pl.when(live)
        def _():
            @pl.loop(0, FRONT_SLOTS // 2)
            def _(pair):
                spot = [phase * FRONT_SLOTS + 2 * pair + t for t in range(2)]
                term = [plan[0, n] for n in spot]
                add_pair(
                    [lambda s: tiles[phase, pl.ds(s, 2)]] * 2,
                    [rights[i] for i in term],
                    mpo_ref, term,
                    [lefts[i] for i in term],
                    [plan[1, n].astype(jnp.float32) for n in spot],
                    held, mixed, acc,
                )

    late = ((odd & there[1]) | (even & there[0]), 1 - near), (there[2], 2), (there[3], 3)
    for live, slot in late:
        pl.when(live)(lambda slot=slot: arrive(slot))
    for live, slot in late:
        pl.when(live)(lambda slot=slot: passing(slot).wait())
    for live, copy in first + second:
        pl.when(live)(lambda copy=copy: copy().wait_send())


SMEM_SPEC = pl.BlockSpec(memory_space=pltpu.SMEM)
VMEM_SPEC = pl.BlockSpec(memory_space=pltpu.VMEM)
ANY_SPEC = pl.BlockSpec(memory_space=pl.ANY)


def front(term_class, psi, left, right, mpo, sectors):
    states, rows, width = psi.shape
    slots = len(STEPS)
    return pl.pallas_call(
        functools.partial(front_kernel, sectors),
        out_shape=(
            jax.ShapeDtypeStruct((slots + 2, *psi.shape), psi.dtype),
            jax.ShapeDtypeStruct(psi.shape, jnp.float32),
        ),
        in_specs=[SMEM_SPEC, ANY_SPEC, ANY_SPEC, ANY_SPEC, VMEM_SPEC],
        out_specs=(ANY_SPEC, VMEM_SPEC),
        scratch_shapes=[
            pltpu.VMEM((FRONT_KINDS, states, rows, width), jnp.bfloat16),
            pltpu.VMEM(left.shape, jnp.bfloat16),
            pltpu.VMEM(right.shape, jnp.bfloat16),
            pltpu.VMEM((states, rows, 2 * width), jnp.bfloat16),
            pltpu.VMEM((2, states, rows, width), jnp.bfloat16),
            pltpu.SMEM((2, FRONT_KINDS * FRONT_SLOTS), jnp.int32),
        ] + [pltpu.SemaphoreType.DMA((slots + 2,))] * 5,
        compiler_params=pltpu.CompilerParams(collective_id=0, has_side_effects=True, vmem_limit_bytes=VMEM_LIMIT),
        name="front",
    )(term_class, psi, left, right, mpo)


def rest_kernel(sectors, class_ref, psi_ref, got_ref, left_ref, right_ref, mpo_ref, total_ref, own_ref, sent_ref,
                tiles, lefts, rights, acc, held, mixed, plan, tile_sem, left_sem, right_sem, acc_sem):
    sector, core = lax.axis_index("sector"), lax.axis_index("term")
    terms = left_ref.shape[0]
    states = acc.shape[0]
    start = pltpu.make_async_copy(total_ref, acc, acc_sem)
    near = 2 - lax.rem(sector, 2)
    used = jnp.int32(0)
    need = []
    for kind in range(len(STEPS) + 1):
        there = jnp.bool_(True) if kind == 0 else has_source(sector, sectors, STEPS[kind - 1])
        skip = FRONT_SLOTS if kind == 0 else jnp.where(near == kind, FRONT_SLOTS, 0)
        before = used

        def note(index, state, kind=kind, there=there, skip=skip):
            used, found = state
            match = (class_ref[index] == kind) & there
            plan[0, used] = index
            plan[1, used] = kind
            take = match & (found >= skip)
            return used + take.astype(jnp.int32), found + match.astype(jnp.int32)

        used, found = lax.fori_loop(0, terms, note, (used, jnp.int32(0)), unroll=True)
        need.append(used > before)
    plan[0, used] = 0
    plan[1, used] = plan[1, jnp.maximum(used - 1, 0)]
    padded = 2 * ((used + 1) // 2)

    def tile_copy(kind):
        source = psi_ref if kind == 0 else got_ref.at[kind - 1]
        return pltpu.make_async_copy(source, tiles.at[kind], tile_sem.at[kind])

    def side_copies(n):
        term = plan[0, n]
        return (pltpu.make_async_copy(left_ref.at[term], lefts.at[n], left_sem.at[n]),
                pltpu.make_async_copy(right_ref.at[term], rights.at[n], right_sem.at[n]))

    for kind, wanted in enumerate(need):
        pl.when(wanted)(lambda kind=kind: tile_copy(kind).start())

    @pl.loop(0, padded)
    def _(n):
        for copy in side_copies(n):
            copy.start()

    start.start()
    pl.when(padded == 0)(lambda: start.wait())

    @pl.loop(0, padded // 2)
    def _(pair):
        spot = [2 * pair + t for t in range(2)]
        kind = [plan[1, n] for n in spot]
        for n, k in zip(spot, kind):
            for copy in side_copies(n):
                copy.wait()

            @pl.when((n == 0) | (k != plan[1, jnp.maximum(n - 1, 0)]))
            def _():
                pltpu.make_async_copy(psi_ref, tiles.at[k], tile_sem.at[k]).wait()

        add_pair(
            [lambda s, k=k: tiles[k, pl.ds(s, 2)] for k in kind],
            [rights[n] for n in spot],
            mpo_ref, [plan[0, n] for n in spot],
            [lefts[n] for n in spot],
            [(n < used).astype(jnp.float32) for n in spot],
            held, mixed, acc, lambda: pl.when(pair == 0)(lambda: start.wait()),
        )

    half = states // 2
    own_ref[...] = acc[pl.ds(core * half, half)]
    sent_ref[...] = acc[pl.ds((1 - core) * half, half)].astype(sent_ref.dtype)


def rest(term_class, psi, got, left, right, mpo, total, sectors):
    states, rows, width = psi.shape
    terms = left.shape[0]
    half = (states // 2, rows, width)
    return pl.pallas_call(
        functools.partial(rest_kernel, sectors),
        out_shape=(jax.ShapeDtypeStruct(half, jnp.float32), jax.ShapeDtypeStruct(half, jnp.bfloat16)),
        in_specs=[SMEM_SPEC, ANY_SPEC, ANY_SPEC, ANY_SPEC, ANY_SPEC, VMEM_SPEC, ANY_SPEC],
        out_specs=(VMEM_SPEC, VMEM_SPEC),
        scratch_shapes=[
            pltpu.VMEM((len(STEPS) + 1, states, rows, width), jnp.bfloat16),
            pltpu.VMEM((terms + 1, *left.shape[1:]), jnp.bfloat16),
            pltpu.VMEM((terms + 1, *right.shape[1:]), jnp.bfloat16),
            pltpu.VMEM((states, rows, width), jnp.float32),
            pltpu.VMEM((states, rows, 2 * width), jnp.bfloat16),
            pltpu.VMEM((2, states, rows, width), jnp.bfloat16),
            pltpu.SMEM((2, terms + 2), jnp.int32),
            pltpu.SemaphoreType.DMA((len(STEPS) + 1,)),
            pltpu.SemaphoreType.DMA((terms + 1,)),
            pltpu.SemaphoreType.DMA((terms + 1,)),
            pltpu.SemaphoreType.DMA(()),
        ],
        compiler_params=pltpu.CompilerParams(vmem_limit_bytes=VMEM_LIMIT),
        name="rest",
    )(term_class, psi, got, left, right, mpo, total)


def swap_kernel(sent_ref, inbox_ref, sems):
    group, sector, core = (lax.axis_index(name) for name in ("groups", "sector", "term"))
    sibling = (group, sector, 1 - core)
    barrier = pltpu.get_barrier_semaphore()
    pl.semaphore_signal(barrier, inc=1, device_id=sibling, device_id_type=MESH)
    pl.semaphore_wait(barrier, 1)
    copy = pltpu.make_async_remote_copy(
        src_ref=sent_ref, dst_ref=inbox_ref, send_sem=sems.at[0], recv_sem=sems.at[1],
        device_id=sibling, device_id_type=MESH,
    )
    copy.start()
    copy.wait()


def swapped(sent):
    return pl.pallas_call(
        swap_kernel,
        out_shape=jax.ShapeDtypeStruct(sent.shape, sent.dtype),
        in_specs=[ANY_SPEC],
        out_specs=ANY_SPEC,
        scratch_shapes=[pltpu.SemaphoreType.DMA((2,))],
        compiler_params=pltpu.CompilerParams(collective_id=1, has_side_effects=True, vmem_limit_bytes=VMEM_LIMIT),
        name="swap",
    )(sent)


def shards(psi_tiles, env_left, env_right, mpo_local, term_class):
    sectors = lax.axis_size("sector")
    psi, left, right = psi_tiles[0], env_left[0], env_right[0]
    mpo = jnp.transpose(mpo_local, (1, 2, 0))
    got, total = front(term_class, psi, left, right, mpo, sectors)
    own, sent = rest(term_class, psi, got, left, right, mpo, total, sectors)
    return (own + swapped(sent).astype(jnp.float32)).astype(jnp.bfloat16)[None]


def solution(mesh):
    placed = (
        P(("groups", "sector"), None, None, None),
        P(("groups", "sector"), "term", None, None),
        P(("groups", "sector"), "term", None, None),
        P(("groups", "term"), None, None),
        P(("groups", "term")),
    )
    return jax.shard_map(
        shards,
        mesh=mesh,
        in_specs=placed,
        out_specs=P(("groups", "sector"), "term", None, None),
        check_vma=False,
    )
```

```python
import functools

import jax
import jax.numpy as jnp
from jax import lax
from jax.experimental import pallas as pl
from jax.experimental.pallas import tpu as pltpu
from jax.sharding import PartitionSpec as P

GRID = 4
MESH = pl.DeviceIdType.MESH
STEPS = (-1, 1, -GRID, GRID)
FRONT_KINDS, FRONT_SLOTS = 2, 8
VMEM_LIMIT = 56 * 1024 * 1024


def has_source(sector, sectors, step):
    column = lax.rem(sector + 1, GRID)
    if step == -1:
        return (sector >= 1) & (column > 0)
    if step == 1:
        return (sector + 1 < sectors) & (column < GRID - 1)
    if step < 0:
        return sector + step >= 0
    return sector + step < sectors


def add_pair(xs, rights, mpo_ref, terms, lefts, scales, held, mixed, acc):
    states, rows, width = acc.shape
    step = 16
    wide = states * step
    index = lambda axis: lax.broadcasted_iota(jnp.int32, (wide, wide), axis)
    same = lax.rem(index(0), step) == lax.rem(index(1), step)
    entry = lambda axis: lax.broadcasted_iota(jnp.int32, (states * states, wide), axis)
    column = lax.rem(entry(0), states) == entry(1) // step
    spread = (lax.broadcasted_iota(jnp.int32, (wide, states * states), 0) // step
              == lax.broadcasted_iota(jnp.int32, (wide, states * states), 1) // states).astype(jnp.bfloat16)
    flat = mpo_ref[...].reshape(states * states, mpo_ref.shape[2]).astype(jnp.float32)
    number = lax.broadcasted_iota(jnp.int32, flat.shape, 1)

    def dot(a, b):
        return jnp.dot(a, b, preferred_element_type=jnp.float32)

    krons = []
    for term, scale in zip(terms, scales):
        values = jnp.sum(jnp.where(number == term, flat, 0.0), 1, keepdims=True) * scale
        wide_rows = jnp.where(column, values, 0.0).astype(jnp.bfloat16)
        krons.append(jnp.where(same, dot(spread, wide_rows), 0.0).astype(jnp.bfloat16))
    zero = jnp.zeros((width, width), jnp.bfloat16)
    right = jnp.concatenate(
        [jnp.concatenate([rights[0], zero], 1), jnp.concatenate([zero, rights[1]], 1)], 0
    )
    for s in range(0, states, 2):
        x = jnp.concatenate([x(s).reshape(2 * rows, width) for x in xs], 1)
        held[pl.ds(s, 2)] = dot(x, right).astype(jnp.bfloat16).reshape(2, rows, 2 * width)
    for t in range(2):
        for r in range(0, rows, 2 * step):
            part = [
                held[:, pl.ds(r + o, step), pl.ds(t * width, width)].reshape(wide, width) for o in (0, step)
            ]
            out = dot(krons[t], jnp.concatenate(part, 1)).astype(jnp.bfloat16)
            for n, o in enumerate((0, step)):
                mixed[t, :, pl.ds(r + o, step), :] = out[:, n * width:(n + 1) * width].reshape(states, step, width)
    left = jnp.concatenate(lefts, 1)
    for s in range(0, states, 2):
        part = [jnp.concatenate([mixed[t, s], mixed[t, s + 1]], 1) for t in range(2)]
        out = dot(left, jnp.concatenate(part, 0))
        for n in range(2):
            acc[s + n] += out[:, n * width:(n + 1) * width]


def front_kernel(sectors, class_ref, psi_ref, left_ref, right_ref, mpo_ref, got_ref, acc,
                 tiles, lefts, rights, held, mixed, plan, send_sem, recv_sem, pass_sem, got_sem, local_sem):
    group, sector, core = (lax.axis_index(name) for name in ("groups", "sector", "term"))
    half = psi_ref.shape[0] // 2
    terms = left_ref.shape[0]
    mine = pl.ds(core * half, half)
    barrier = pltpu.get_barrier_semaphore()
    sibling = (group, sector, 1 - core)
    assert sectors % 2 == 0
    there = [has_source(sector, sectors, step) for step in STEPS]
    odd = lax.rem(sector, 2) == 1
    even = jnp.logical_not(odd)
    above, below = sector + 2 < sectors, sector >= 2
    partner = jnp.where(odd, sector - 1, sector + 1)
    near = jnp.where(odd, 0, 1)
    near_there = (odd & there[0]) | (even & there[1])
    up_out = above & ((sector + 4 < sectors) | (odd & there[1]))
    up_in = below & (above | (odd & has_source(sector - 2, sectors, 1)))
    down_out = below & ((sector >= 4) | (even & there[0]))
    down_in = above & (below | (even & has_source(sector + 2, sectors, -1)))
    across_0 = odd & below & has_source(sector - 1, sectors, -1)
    across_1 = even & above & has_source(sector + 1, sectors, 1)
    through = above & below

    def greet(target):
        pl.semaphore_signal(barrier, inc=1, device_id=target, device_id_type=MESH)

    greet(sibling)
    greet((group, partner, core))
    pl.when(above)(lambda: greet((group, sector + 2, core)))
    pl.when(below)(lambda: greet((group, sector - 2, core)))
    pl.semaphore_wait(barrier, 2 + above.astype(jnp.int32) + below.astype(jnp.int32))

    def send(source, slot, target):
        return pltpu.make_async_remote_copy(
            src_ref=source,
            dst_ref=got_ref.at[slot, mine],
            send_sem=send_sem.at[slot],
            recv_sem=recv_sem.at[slot],
            device_id=(group, target, core),
            device_id_type=MESH,
        )

    tile, lower, upper = psi_ref.at[mine], got_ref.at[4, mine], got_ref.at[5, mine]
    first = (
        (up_out, lambda: send(tile, 4, sector + 2)),
        (down_out, lambda: send(tile, 5, sector - 2)),
        (near_there, lambda: send(tile, 1 - near, partner)),
    )
    second = (
        (across_0, lambda: send(lower, 0, partner)),
        (through, lambda: send(lower, 2, sector + 2)),
        (across_1, lambda: send(upper, 1, partner)),
        (through, lambda: send(upper, 3, sector - 2)),
    )

    def passing(slot):
        return pltpu.make_async_remote_copy(
            src_ref=got_ref.at[slot, mine],
            dst_ref=got_ref.at[slot, mine],
            send_sem=pass_sem.at[slot],
            recv_sem=got_sem.at[slot],
            device_id=sibling,
            device_id_type=MESH,
        )

    def arrive(slot):
        send(tile, slot, partner).wait_recv()
        passing(slot).start()

    for live, copy in first:
        pl.when(live)(lambda copy=copy: copy().start())
    copies = [
        pltpu.make_async_copy(psi_ref, tiles.at[0], local_sem.at[0]),
        pltpu.make_async_copy(left_ref, lefts, local_sem.at[1]),
        pltpu.make_async_copy(right_ref, rights, local_sem.at[2]),
    ]
    for copy in copies:
        copy.start()

    def note(index, state):
        fresh = []
        for kind, (found, slots) in enumerate(state):
            match = class_ref[index] == (0 if kind == 0 else near + 1)
            slots = tuple(jnp.where(match & (found == n), index, slot) for n, slot in enumerate(slots))
            fresh.append((found + match.astype(jnp.int32), slots))
        return tuple(fresh)

    zero = jnp.int32(0)
    state = lax.fori_loop(0, terms, note, tuple((zero, (zero,) * FRONT_SLOTS) for _ in range(FRONT_KINDS)))
    for kind, (found, slots) in enumerate(state):
        for n, slot in enumerate(slots):
            plan[0, kind * FRONT_SLOTS + n] = slot
            plan[1, kind * FRONT_SLOTS + n] = (n < found).astype(jnp.int32)
    acc[...] = jnp.zeros_like(acc)
    for copy in copies:
        copy.wait()

    @pl.loop(0, FRONT_KINDS)
    def _(phase):
        @pl.when(phase == 1)
        def _():
            @pl.when(up_in)
            def _():
                send(tile, 4, partner).wait_recv()
                for live, copy in second[:2]:
                    pl.when(live)(lambda copy=copy: copy().start())

            @pl.when(down_in)
            def _():
                send(tile, 5, partner).wait_recv()
                for live, copy in second[2:]:
                    pl.when(live)(lambda copy=copy: copy().start())

            @pl.when(near_there)
            def _():
                arrive(near)
                passing(near).wait()
                copy = pltpu.make_async_copy(got_ref.at[near], tiles.at[1], local_sem.at[3])
                copy.start()
                copy.wait()

        live = (phase == 0) | near_there

        @pl.when(live)
        def _():
            @pl.loop(0, FRONT_SLOTS // 2)
            def _(pair):
                spot = [phase * FRONT_SLOTS + 2 * pair + t for t in range(2)]
                term = [plan[0, n] for n in spot]
                add_pair(
                    [lambda s: tiles[phase, pl.ds(s, 2)]] * 2,
                    [rights[i] for i in term],
                    mpo_ref, term,
                    [lefts[i] for i in term],
                    [plan[1, n].astype(jnp.float32) for n in spot],
                    held, mixed, acc,
                )

    late = ((odd & there[1]) | (even & there[0]), 1 - near), (there[2], 2), (there[3], 3)
    for live, slot in late:
        pl.when(live)(lambda slot=slot: arrive(slot))
    for live, slot in late:
        pl.when(live)(lambda slot=slot: passing(slot).wait())
    for live, copy in first + second:
        pl.when(live)(lambda copy=copy: copy().wait_send())


SMEM_SPEC = pl.BlockSpec(memory_space=pltpu.SMEM)
VMEM_SPEC = pl.BlockSpec(memory_space=pltpu.VMEM)
ANY_SPEC = pl.BlockSpec(memory_space=pl.ANY)


def front(term_class, psi, left, right, mpo, sectors):
    states, rows, width = psi.shape
    slots = len(STEPS)
    return pl.pallas_call(
        functools.partial(front_kernel, sectors),
        out_shape=(
            jax.ShapeDtypeStruct((slots + 2, *psi.shape), psi.dtype),
            jax.ShapeDtypeStruct(psi.shape, jnp.float32),
        ),
        in_specs=[SMEM_SPEC, ANY_SPEC, ANY_SPEC, ANY_SPEC, VMEM_SPEC],
        out_specs=(ANY_SPEC, VMEM_SPEC),
        scratch_shapes=[
            pltpu.VMEM((FRONT_KINDS, states, rows, width), jnp.bfloat16),
            pltpu.VMEM(left.shape, jnp.bfloat16),
            pltpu.VMEM(right.shape, jnp.bfloat16),
            pltpu.VMEM((states, rows, 2 * width), jnp.bfloat16),
            pltpu.VMEM((2, states, rows, width), jnp.bfloat16),
            pltpu.SMEM((2, FRONT_KINDS * FRONT_SLOTS), jnp.int32),
        ] + [pltpu.SemaphoreType.DMA((slots + 2,))] * 5,
        compiler_params=pltpu.CompilerParams(collective_id=0, has_side_effects=True, vmem_limit_bytes=VMEM_LIMIT),
        name="front",
    )(term_class, psi, left, right, mpo)


def rest_kernel(sectors, class_ref, psi_ref, got_ref, left_ref, right_ref, mpo_ref, total_ref, own_ref, sent_ref,
                tiles, lefts, rights, acc, held, mixed, plan, tile_sem, left_sem, right_sem, acc_sem):
    sector, core = lax.axis_index("sector"), lax.axis_index("term")
    terms = left_ref.shape[0]
    states = acc.shape[0]
    start = pltpu.make_async_copy(total_ref, acc, acc_sem)
    start.start()
    near = 2 - lax.rem(sector, 2)
    used = jnp.int32(0)
    need = []
    for kind in range(len(STEPS) + 1):
        there = jnp.bool_(True) if kind == 0 else has_source(sector, sectors, STEPS[kind - 1])
        skip = FRONT_SLOTS if kind == 0 else jnp.where(near == kind, FRONT_SLOTS, 0)
        before = used

        def note(index, state, kind=kind, there=there, skip=skip):
            used, found = state
            match = (class_ref[index] == kind) & there
            plan[0, used] = index
            plan[1, used] = kind
            take = match & (found >= skip)
            return used + take.astype(jnp.int32), found + match.astype(jnp.int32)

        used, found = lax.fori_loop(0, terms, note, (used, jnp.int32(0)), unroll=True)
        need.append(used > before)
    plan[0, used] = 0
    plan[1, used] = plan[1, jnp.maximum(used - 1, 0)]
    padded = 2 * ((used + 1) // 2)

    def tile_copy(kind):
        source = psi_ref if kind == 0 else got_ref.at[kind - 1]
        return pltpu.make_async_copy(source, tiles.at[kind], tile_sem.at[kind])

    def side_copies(n):
        term = plan[0, n]
        return (pltpu.make_async_copy(left_ref.at[term], lefts.at[n], left_sem.at[n]),
                pltpu.make_async_copy(right_ref.at[term], rights.at[n], right_sem.at[n]))

    for kind, wanted in enumerate(need):
        pl.when(wanted)(lambda kind=kind: tile_copy(kind).start())

    @pl.loop(0, padded)
    def _(n):
        for copy in side_copies(n):
            copy.start()

    start.wait()
    for kind, wanted in enumerate(need):
        pl.when(wanted)(lambda kind=kind: tile_copy(kind).wait())

    @pl.loop(0, padded // 2)
    def _(pair):
        spot = [2 * pair + t for t in range(2)]
        for n in spot:
            for copy in side_copies(n):
                copy.wait()
        kind = [plan[1, n] for n in spot]
        add_pair(
            [lambda s, k=k: tiles[k, pl.ds(s, 2)] for k in kind],
            [rights[n] for n in spot],
            mpo_ref, [plan[0, n] for n in spot],
            [lefts[n] for n in spot],
            [(n < used).astype(jnp.float32) for n in spot],
            held, mixed, acc,
        )

    half = states // 2
    own_ref[...] = acc[pl.ds(core * half, half)].astype(own_ref.dtype)
    sent_ref[...] = acc[pl.ds((1 - core) * half, half)].astype(sent_ref.dtype)


def rest(term_class, psi, got, left, right, mpo, total, sectors):
    states, rows, width = psi.shape
    terms = left.shape[0]
    half = (states // 2, rows, width)
    return pl.pallas_call(
        functools.partial(rest_kernel, sectors),
        out_shape=(jax.ShapeDtypeStruct(half, jnp.bfloat16), jax.ShapeDtypeStruct(half, jnp.bfloat16)),
        in_specs=[SMEM_SPEC, ANY_SPEC, ANY_SPEC, ANY_SPEC, ANY_SPEC, VMEM_SPEC, ANY_SPEC],
        out_specs=(VMEM_SPEC, VMEM_SPEC),
        scratch_shapes=[
            pltpu.VMEM((len(STEPS) + 1, states, rows, width), jnp.bfloat16),
            pltpu.VMEM((terms + 1, *left.shape[1:]), jnp.bfloat16),
            pltpu.VMEM((terms + 1, *right.shape[1:]), jnp.bfloat16),
            pltpu.VMEM((states, rows, width), jnp.float32),
            pltpu.VMEM((states, rows, 2 * width), jnp.bfloat16),
            pltpu.VMEM((2, states, rows, width), jnp.bfloat16),
            pltpu.SMEM((2, terms + 2), jnp.int32),
            pltpu.SemaphoreType.DMA((len(STEPS) + 1,)),
            pltpu.SemaphoreType.DMA((terms + 1,)),
            pltpu.SemaphoreType.DMA((terms + 1,)),
            pltpu.SemaphoreType.DMA(()),
        ],
        compiler_params=pltpu.CompilerParams(vmem_limit_bytes=VMEM_LIMIT),
        name="rest",
    )(term_class, psi, got, left, right, mpo, total)


def swap_kernel(sent_ref, inbox_ref, sems):
    group, sector, core = (lax.axis_index(name) for name in ("groups", "sector", "term"))
    sibling = (group, sector, 1 - core)
    barrier = pltpu.get_barrier_semaphore()
    pl.semaphore_signal(barrier, inc=1, device_id=sibling, device_id_type=MESH)
    pl.semaphore_wait(barrier, 1)
    copy = pltpu.make_async_remote_copy(
        src_ref=sent_ref, dst_ref=inbox_ref, send_sem=sems.at[0], recv_sem=sems.at[1],
        device_id=sibling, device_id_type=MESH,
    )
    copy.start()
    copy.wait()


def swapped(sent):
    return pl.pallas_call(
        swap_kernel,
        out_shape=jax.ShapeDtypeStruct(sent.shape, sent.dtype),
        in_specs=[ANY_SPEC],
        out_specs=ANY_SPEC,
        scratch_shapes=[pltpu.SemaphoreType.DMA((2,))],
        compiler_params=pltpu.CompilerParams(collective_id=1, has_side_effects=True, vmem_limit_bytes=VMEM_LIMIT),
        name="swap",
    )(sent)


def shards(psi_tiles, env_left, env_right, mpo_local, term_class):
    sectors = lax.axis_size("sector")
    psi, left, right = psi_tiles[0], env_left[0], env_right[0]
    mpo = jnp.transpose(mpo_local, (1, 2, 0))
    got, total = front(term_class, psi, left, right, mpo, sectors)
    own, sent = rest(term_class, psi, got, left, right, mpo, total, sectors)
    return (own.astype(jnp.float32) + swapped(sent).astype(jnp.float32)).astype(jnp.bfloat16)[None]


def solution(mesh):
    placed = (
        P(("groups", "sector"), None, None, None),
        P(("groups", "sector"), "term", None, None),
        P(("groups", "sector"), "term", None, None),
        P(("groups", "term"), None, None),
        P(("groups", "term")),
    )
    return jax.shard_map(
        shards,
        mesh=mesh,
        in_specs=placed,
        out_specs=P(("groups", "sector"), "term", None, None),
        check_vma=False,
    )
```
